256 devices in a mesh: section: 2 (over x_lo), tensor: 128 (over y, z, x_hi, core).
Axes of the slice: x: 4 (x_hi: 2, x_lo: 2; x = x_hi * 2 + x_lo), y: 4, z: 8, core: 2. Of those that a mesh axis runs over, the one named last changes fastest.
Arguments:
- resid_in: bfloat16 [256, 8192], P(None, 'tensor'), may hold values from -6 to 6
- contexts: bfloat16 [2, 256, 16384], P('section', None, 'tensor'), may hold values from -6 to 6
- out_proj: bfloat16 [2, 16384, 8192], P('section', 'tensor'), may hold values from -0.046875 to 0.046875
- encoder: bfloat16 [8192, 32768], P(None, ('section', 'tensor')), may hold values from -0.0625 to 0.0625
- enc_bias: bfloat16 [32768], P(('section', 'tensor')), may hold values from -3 to 3
- decoder: bfloat16 [32768, 8192], P(('section', 'tensor')), may hold values from -0.125 to 0.125
- dec_bias: bfloat16 [8192], replicated, may hold values from -3 to 3
- token_ids: int32 [256], replicated, may hold values from 0 to 128000, as said below
- owner_map: int32 [128], replicated, may hold values from 0 to 127, each once
Outputs:
- owned_error: bfloat16 [256, 8192], P('tensor', 'section')
- new_encoder: bfloat16 [8192, 32768], P(None, ('section', 'tensor'))
- new_decoder: bfloat16 [32768, 8192], P(('section', 'tensor'))
The draws below stay inside these ranges and needn't reach their ends.
Inputs may be any that keep to these rules, and one draw needn't show every extreme that they name: `token_ids`: 128000 marks a document start and stands at the first token of every micro-batch; all other ids lie below 128000.
All inputs are finite; a program needn't handle non-finite values.
Results may differ from the reference program's by a relative error of at most 0.02005.
Values may be sent and summed in bfloat16 or wider, within the bound.
No kernel may reach another device: no remote copies, remote signals or barrier semaphores. Data moves between devices by JAX's collectives and lax.ppermute only.
A program may use at most 128 MiB of HBM per device.

```python
import jax
import jax.numpy as jnp
from jax import lax

D = 8192
HD = 16384
LAT = 32768
MICRO = 2
MROWS = 128
BOS = 128000
TOK = 256
BLOCKS = 128


def draw_token_ids(key, part):
    key = jax.random.fold_in(key, 7)
    first_key, second_key = jax.random.split(key)
    drawn_ids = jax.random.randint(first_key, (MICRO, MROWS), 0, BOS)
    starting = jax.random.randint(second_key, (MICRO, MROWS), 0, 16) == 0
    leading = jnp.arange(MROWS)[None, :] == 0
    token_ids = jnp.where(starting | leading, BOS, drawn_ids)
    return token_ids.reshape(MICRO * MROWS).astype(jnp.int32)


def spiked(drawn, own_key, source, target, blocks, factor):
    owner, partner = [(jnp.arange(drawn.shape[axis_at]) // (drawn.shape[axis_at] // blocks)).reshape([-1 if axis == axis_at else 1 for axis in range(drawn.ndim)]) for axis_at in (source, target)]
    chosen = jax.random.permutation(own_key, blocks)[partner]
    strong = (owner == chosen) | (owner == (partner + blocks // 2) % blocks)
    return jnp.where(strong, factor * drawn, drawn)


def shard_levels(rng, dims, cuts, smallest, high):
    def one(position, blocks):
        draws = jax.random.uniform(jax.random.fold_in(jax.random.fold_in(rng, 6), position), (blocks,), jnp.float32, smallest / len(cuts), high / len(cuts))
        return jnp.repeat(jnp.exp(draws), dims[position] // blocks).reshape((-1,) + (1,) * (len(dims) - position - 1))

    factor_of = one(*cuts[0])
    for cut in cuts[1:]:
        factor_of = factor_of * one(*cut)
    return factor_of


def bell_draw(rng, dims, width, bound, pieces=(), kind=jnp.bfloat16):
    loudness = shard_levels(rng, dims, pieces, -0.22, 0.18) if pieces else 1.0
    values = jax.random.normal(rng, dims, jnp.float32) * width * loudness
    return jnp.minimum(jnp.maximum(values, -bound), bound).astype(kind)


def bell_draw_with(own_key, extent, scale, most, cuts, heavy, held_as=jnp.bfloat16):
    entries = scale * jax.random.normal(own_key, extent, jnp.float32)
    if cuts:
        entries = entries * shard_levels(own_key, extent, cuts, -0.22, 0.18)
    return jnp.clip(spiked(entries, jax.random.fold_in(own_key, 3), *heavy), -most, most).astype(held_as)


def setup_inputs(seed: int = 0) -> dict:
    streams_of = jax.random.split(jax.random.key(seed), 10)
    resid_in = bell_draw(streams_of[0], (TOK, D), 1.0, 6.0, ((1, 128),))
    contexts = bell_draw(streams_of[1], (2, TOK, HD), 1.0, 6.0, ((0, 2), (2, 128)))
    out_proj = bell_draw(streams_of[2], (2, HD, D), HD ** -0.5, 0.046875, ((0, 2), (1, 128)))
    encoder = bell_draw(streams_of[3], (D, LAT), D ** -0.5, 0.0625, ((1, 256),))
    enc_bias = bell_draw(streams_of[4], (LAT,), 0.5, 3.0, ((0, 256),))
    decoder = bell_draw_with(streams_of[5], (LAT, D), LAT ** -0.5, 0.125, ((0, 256),), (0, 1, 256, 6.0))
    dec_bias = bell_draw(streams_of[6], (D,), 0.5, 3.0)
    token_ids = draw_token_ids(jax.random.fold_in(streams_of[9], 71), 0)
    owner_map = jax.random.permutation(streams_of[8], BLOCKS).astype(jnp.int32)
    return {"resid_in": resid_in, "contexts": contexts, "out_proj": out_proj, "encoder": encoder, "enc_bias": enc_bias, "decoder": decoder, "dec_bias": dec_bias, "token_ids": token_ids, "owner_map": owner_map}


STEP_RATE = 0.5

def reference(resid_in, contexts, out_proj, encoder, enc_bias, decoder, dec_bias, token_ids, owner_map):
    resid_mid = (resid_in.astype(jnp.float32) + jnp.dot(contexts[0], out_proj[0], preferred_element_type=jnp.float32)).astype(jnp.bfloat16)
    resid_last = (resid_mid.astype(jnp.float32) + jnp.dot(contexts[1], out_proj[1], preferred_element_type=jnp.float32)).astype(jnp.bfloat16)
    last_values = resid_last.astype(jnp.float32)
    inverse_rms = lax.rsqrt(lax.optimization_barrier(jnp.mean(last_values * last_values, axis=1, keepdims=True)) + 1e-05)
    centred = (last_values * inverse_rms - dec_bias.astype(jnp.float32)).astype(jnp.bfloat16)
    before_relu = jnp.dot(centred, encoder, preferred_element_type=jnp.float32) + enc_bias.astype(jnp.float32)
    latents = jnp.maximum(before_relu, 0.0).astype(jnp.bfloat16)
    kept_rows = (token_ids != BOS).astype(jnp.float32)[:, None]
    rebuilt = jnp.dot(latents, decoder, preferred_element_type=jnp.float32)
    error_rows = (kept_rows * (rebuilt - centred.astype(jnp.float32))).astype(jnp.bfloat16)
    block_rows = TOK // BLOCKS
    grouped = error_rows.reshape(BLOCKS, block_rows, D)
    owned_error = jnp.zeros_like(grouped).at[owner_map].set(grouped).reshape(TOK, D)
    grad_dec = jnp.dot(latents.T, error_rows, preferred_element_type=jnp.float32)
    backward = jnp.dot(error_rows, decoder.T, preferred_element_type=jnp.float32)
    pre_grad = jnp.where(before_relu > 0.0, backward, 0.0).astype(jnp.bfloat16)
    grad_enc = jnp.dot(centred.T, pre_grad, preferred_element_type=jnp.float32)
    step_size = STEP_RATE / TOK
    new_encoder = (encoder.astype(jnp.float32) - step_size * grad_enc).astype(jnp.bfloat16)
    new_decoder = (decoder.astype(jnp.float32) - step_size * grad_dec).astype(jnp.bfloat16)
    return (owned_error, new_encoder, new_decoder)
```

```python
import jax
import jax.numpy as jnp
from jax import lax
from jax.sharding import Mesh
from jax.sharding import PartitionSpec as P

BOS = 128000


STEP_RATE = 0.5

AXES = ("xl", "y", "z", "xh", "c")
PLANE = ("y", "xh", "xl")
TENSOR = ("y", "z", "xh", "c")


def exchange(value, swap):
    sizes = [lax.axis_size(a) for a in AXES]
    route = []
    for source in range(sizes[0] * sizes[1] * sizes[2] * sizes[3] * sizes[4]):
        rest, place = source, {}
        for axis, size in zip(AXES[::-1], sizes[::-1]):
            place[axis] = rest % size
            rest //= size
        place = swap(place)
        target = 0
        for axis, size in zip(AXES, sizes):
            target = target * size + place[axis]
        route.append((source, target))
    return lax.ppermute(value, AXES, route)


def other_core(value):
    return exchange(value, lambda p: {**p, "c": 1 - p["c"]})


def core_and_section(value):
    return exchange(value, lambda p: {**p, "c": p["xl"], "xl": p["c"]})


def reduce_rows(partial, plane, depth):
    width = partial.shape[1]
    pieces = lax.all_to_all(partial.reshape(plane, -1, width), PLANE, 0, 0, tiled=True)
    chunk = jnp.sum(pieces.astype(jnp.float32), axis=0).astype(jnp.bfloat16)
    pieces = lax.all_to_all(chunk.reshape(depth, -1, width), "z", 0, 0, tiled=True)
    return jnp.sum(pieces.astype(jnp.float32), axis=0)


def gather_rows(rows, plane, depth):
    width = rows.shape[1]
    rows = lax.all_to_all(
        jnp.broadcast_to(rows[None], (depth,) + rows.shape), "z", 0, 0, tiled=True
    ).reshape(-1, width)
    return lax.all_to_all(
        jnp.broadcast_to(rows[None], (plane,) + rows.shape), PLANE, 0, 0, tiled=True
    ).reshape(-1, width)


def matmul(a, b, dims=((1,), (0,))):
    return lax.dot_general(a, b, (dims, ((), ())), preferred_element_type=jnp.float32)


def shards(
    resid_in, contexts, out_proj, encoder, enc_bias, decoder, dec_bias, token_ids, owner_map
):
    tokens = resid_in.shape[0]
    features = decoder.shape[1]
    half = features // 2
    blocks = owner_map.shape[0]
    block_rows = tokens // blocks
    depth = lax.axis_size("z")
    plane = lax.axis_size("y") * lax.axis_size("xh") * lax.axis_size("xl")
    y, z, xh, xl, core = (lax.axis_index(a) for a in ("y", "z", "xh", "xl", "c"))
    size_xh, size_xl = lax.axis_size("xh"), lax.axis_size("xl")

    row = lax.broadcasted_iota(jnp.int32, (tokens, tokens), 0)
    old = lax.broadcasted_iota(jnp.int32, (tokens, tokens), 1)
    slot = row // block_rows
    at_z, at_plane = slot % depth, slot // depth
    at_y, at_x = at_plane // (size_xh * size_xl), at_plane % (size_xh * size_xl)
    position = (at_y * depth + at_z) * (size_xh * size_xl) + at_x
    owner_of_row = jnp.repeat(owner_map, block_rows)
    order = (
        (owner_of_row[None, :] == position) & (old % block_rows == row % block_rows)
    ).astype(jnp.bfloat16)
    my_position = ((y * depth + z) * size_xh + xh) * size_xl + xl
    kept = (token_ids.reshape(blocks, block_rows) != BOS).astype(jnp.float32)
    mask_rows = jnp.sum(
        jnp.where((owner_map == my_position)[:, None], kept, 0.0), axis=0
    )[:, None]

    def mine(weight, axis):
        return lax.dynamic_slice_in_dim(weight, core * half, half, axis)

    def theirs(weight, axis):
        return lax.dynamic_slice_in_dim(weight, (1 - core) * half, half, axis)

    proj = out_proj[0]
    proj_other = other_core(theirs(proj, 1))
    dec_other = other_core(theirs(decoder, 1))
    context = matmul(order, contexts[0]).astype(jnp.bfloat16)
    resid = matmul(order, resid_in).astype(jnp.bfloat16)
    context_other = other_core(context)
    resid_other = other_core(resid)

    partial = (matmul(context, mine(proj, 1)) + matmul(context_other, proj_other)).astype(
        jnp.bfloat16
    )
    columns = jnp.where(
        core == 0,
        jnp.concatenate([resid, resid_other], axis=1),
        jnp.concatenate([resid_other, resid], axis=1),
    ).astype(jnp.float32)
    start = ((y * depth + z) * size_xh + xh) * columns.shape[1]
    owns = (start // half == core) & (xl == 0)
    start = start % half
    here = lax.dynamic_slice_in_dim(partial, start, columns.shape[1], 1).astype(jnp.float32)
    partial = lax.dynamic_update_slice_in_dim(
        partial, (here + jnp.where(owns, columns, 0.0)).astype(jnp.bfloat16), start, 1
    )
    values = (
        reduce_rows(partial, plane, depth).astype(jnp.bfloat16).astype(jnp.float32)
    )
    squares = jnp.sum(values * values, axis=1, keepdims=True)
    squares = squares + other_core(squares)
    inverse_rms = lax.rsqrt(squares / features + 1e-05)
    my_centred = (values * inverse_rms - mine(dec_bias, 0).astype(jnp.float32)).astype(
        jnp.bfloat16
    )
    centred = gather_rows(my_centred, plane, depth)
    centred_other = other_core(centred)
    low, high = (
        jnp.where(core == 0, centred, centred_other),
        jnp.where(core == 0, centred_other, centred),
    )
    before_relu = (
        matmul(low, encoder[:half])
        + matmul(high, encoder[half:])
        + enc_bias.astype(jnp.float32)
    )
    latents = jnp.maximum(before_relu, 0.0).astype(jnp.bfloat16)
    latents_other = other_core(latents)
    rebuilt = reduce_rows(
        (matmul(latents, mine(decoder, 1)) + matmul(latents_other, dec_other)).astype(
            jnp.bfloat16
        ),
        plane,
        depth,
    )
    my_error = (mask_rows * (rebuilt - my_centred.astype(jnp.float32))).astype(jnp.bfloat16)
    owned_error = core_and_section(my_error)
    error = gather_rows(my_error, plane, depth)
    error_other = other_core(error)
    error_low, error_high = (
        jnp.where(core == 0, error, error_other),
        jnp.where(core == 0, error_other, error),
    )
    backward = matmul(error_low, decoder[:, :half], ((1,), (1,))) + matmul(
        error_high, decoder[:, half:], ((1,), (1,))
    )
    pre_grad = jnp.where(before_relu > 0.0, backward, 0.0).astype(jnp.bfloat16)
    step_size = STEP_RATE / tokens

    def stepped(weight, grad):
        return (weight.astype(jnp.float32) - step_size * grad).astype(jnp.bfloat16)

    over_rows = ((0,), (0,))
    new_encoder = jnp.concatenate(
        [
            stepped(encoder[:half], matmul(low, pre_grad, over_rows)),
            stepped(encoder[half:], matmul(high, pre_grad, over_rows)),
        ],
        axis=0,
    )
    new_decoder = jnp.concatenate(
        [
            stepped(decoder[:, :half], matmul(latents, error_low, over_rows)),
            stepped(decoder[:, half:], matmul(latents, error_high, over_rows)),
        ],
        axis=1,
    )
    return (owned_error, new_encoder, new_decoder)


def solution(mesh):
    cut = Mesh(mesh.devices.reshape(2, 4, 8, 2, 2), AXES)
    return jax.shard_map(
        shards,
        mesh=cut,
        in_specs=(
            P(None, TENSOR),
            P("xl", None, TENSOR),
            P("xl", TENSOR, None),
            P(None, AXES),
            P(AXES),
            P(AXES, None),
            P(),
            P(),
            P(),
        ),
        out_specs=(
            P(TENSOR, "xl"),
            P(None, AXES),
            P(AXES, None),
        ),
        check_vma=False,
    )
```

```python
import jax
import jax.numpy as jnp
from jax import lax
from jax.sharding import Mesh
from jax.sharding import PartitionSpec as P

BOS = 128000


STEP_RATE = 0.5

AXES = ("xl", "y", "zh", "zl", "xh", "c")
SIZES = (2, 4, 4, 2, 2, 2)
NEAR = ("y", "xh", "xl", "zl")
FAR = "zh"
TENSOR = ("y", "zh", "zl", "xh", "c")


def exchange(value, swap):
    route = []
    for source in range(256):
        rest, place = source, {}
        for axis, size in zip(AXES[::-1], SIZES[::-1]):
            place[axis] = rest % size
            rest //= size
        place = swap(place)
        target = 0
        for axis, size in zip(AXES, SIZES):
            target = target * size + place[axis]
        route.append((source, target))
    return lax.ppermute(value, AXES, route)


def other_core(value):
    return exchange(value, lambda p: {**p, "c": 1 - p["c"]})


def core_and_section(value):
    return exchange(value, lambda p: {**p, "c": p["xl"], "xl": p["c"]})


def matmul(a, b, dims=((1,), (0,))):
    return lax.dot_general(a, b, (dims, ((), ())), preferred_element_type=jnp.float32)


def spread(value, axes, count):
    return lax.all_to_all(
        jnp.broadcast_to(value[None], (count,) + value.shape), axes, 0, 0, tiled=True
    )


def sum_pieces(partial, near, far):
    tokens, width = partial.shape
    depth = tokens // near
    pieces = lax.all_to_all(partial.reshape(near, depth, width), NEAR, 0, 0, tiled=True)
    to = lax.broadcasted_iota(jnp.int32, (depth, tokens), 0)
    of = lax.broadcasted_iota(jnp.int32, (depth, tokens), 1)
    adds = (of % depth == to).astype(jnp.bfloat16)
    chunk = matmul(adds, pieces.reshape(tokens, width)).astype(jnp.bfloat16)
    return jnp.sum(spread(chunk, FAR, far).astype(jnp.float32), axis=0)


def shards(
    resid_in, contexts, out_proj, encoder, enc_bias, decoder, dec_bias, token_ids, owner_map
):
    tokens = resid_in.shape[0]
    features = decoder.shape[1]
    own = decoder.shape[0]
    half = features // 2
    blocks = owner_map.shape[0]
    block_rows = tokens // blocks
    far = lax.axis_size(FAR)
    near = blocks // far
    depth = tokens // near
    y, zh, zl, xh, xl, core = (
        lax.axis_index(a) for a in ("y", "zh", "zl", "xh", "xl", "c")
    )

    row = lax.broadcasted_iota(jnp.int32, (tokens, tokens), 0)
    old = lax.broadcasted_iota(jnp.int32, (tokens, tokens), 1)
    slot = row // block_rows
    position = (
        (slot // 32) * 32 + (slot % 4) * 8 + (slot // 4 % 2) * 4 + (slot // 8 % 4)
    )
    owner_of_row = jnp.repeat(owner_map, block_rows)
    order = (
        (owner_of_row[None, :] == position) & (old % block_rows == row % block_rows)
    ).astype(jnp.bfloat16)
    my_slot = ((y * 2 + xh) * 2 + xl) * 2 + zl
    kept = (token_ids != BOS).astype(jnp.bfloat16)
    mask_rows = lax.dynamic_slice_in_dim(
        matmul(order, kept[:, None]), my_slot * depth, depth, 0
    )

    def mine(weight, axis):
        return lax.dynamic_slice_in_dim(weight, core * half, half, axis)

    def theirs(weight, axis):
        return lax.dynamic_slice_in_dim(weight, (1 - core) * half, half, axis)

    proj = out_proj[0]
    proj_both = jnp.concatenate([mine(proj, 1), other_core(theirs(proj, 1))], axis=0)
    context = matmul(order, contexts[0]).astype(jnp.bfloat16)
    resid = matmul(order, resid_in).astype(jnp.bfloat16)
    context_both = jnp.concatenate([context, other_core(context)], axis=1)
    resid_other = other_core(resid)
    partial = matmul(context_both, proj_both).astype(jnp.bfloat16)
    columns = jnp.where(
        core == 0,
        jnp.concatenate([resid, resid_other], axis=1),
        jnp.concatenate([resid_other, resid], axis=1),
    ).astype(jnp.float32)
    start = (((y * 4 + zh) * 2 + zl) * 2 + xh) * columns.shape[1]
    owns = (start // half == core) & (xl == 0)
    start = start % half
    here = lax.dynamic_slice_in_dim(partial, start, columns.shape[1], 1).astype(jnp.float32)
    partial = lax.dynamic_update_slice_in_dim(
        partial, (here + jnp.where(owns, columns, 0.0)).astype(jnp.bfloat16), start, 1
    )
    values = sum_pieces(partial, near, far).astype(jnp.bfloat16).astype(jnp.float32)
    squares = jnp.sum(values * values, axis=1, keepdims=True)
    squares = squares + other_core(squares)
    inverse_rms = lax.rsqrt(squares / features + 1e-05)
    my_centred = (values * inverse_rms - mine(dec_bias, 0).astype(jnp.float32)).astype(
        jnp.bfloat16
    )
    encoder_both = jnp.concatenate([mine(encoder, 0), other_core(theirs(encoder, 0))], axis=1)
    decoder_both = jnp.concatenate([mine(decoder, 1), other_core(theirs(decoder, 1))], axis=0)
    centred = spread(my_centred, NEAR, near).reshape(tokens, half)
    products = matmul(centred, encoder_both)
    before_relu = (
        products[:, :own]
        + other_core(products[:, own:])
        + enc_bias.astype(jnp.float32)
    )
    latents = jnp.maximum(before_relu, 0.0).astype(jnp.bfloat16)
    latents_both = jnp.concatenate([latents, other_core(latents)], axis=1)
    partial = matmul(latents_both, decoder_both).astype(jnp.bfloat16)
    later, _ = lax.optimization_barrier((centred, partial))
    centred_other = other_core(later)
    centred_full = jnp.where(
        core == 0,
        jnp.concatenate([later, centred_other], axis=1),
        jnp.concatenate([centred_other, later], axis=1),
    )
    rebuilt = sum_pieces(partial, near, far)
    my_error = (mask_rows * (rebuilt - my_centred.astype(jnp.float32))).astype(jnp.bfloat16)
    owned_error = core_and_section(
        lax.dynamic_slice_in_dim(my_error, zh * block_rows, block_rows, 0)
    )
    error = spread(my_error, NEAR, near).reshape(tokens, half)
    step_size = STEP_RATE / tokens

    def stepped(weight, grad):
        return (weight.astype(jnp.float32) - step_size * grad).astype(jnp.bfloat16)

    over_rows = ((0,), (0,))
    products = matmul(error, decoder_both, ((1,), (1,)))
    backward = products[:, :own] + other_core(products[:, own:])
    pre_grad = jnp.where(before_relu > 0.0, backward, 0.0).astype(jnp.bfloat16)
    stepped_both = stepped(decoder_both, matmul(latents_both, error, over_rows))
    kept_half, back_half = stepped_both[:own], other_core(stepped_both[own:])
    new_decoder = jnp.where(
        core == 0,
        jnp.concatenate([kept_half, back_half], axis=1),
        jnp.concatenate([back_half, kept_half], axis=1),
    )
    new_encoder = stepped(encoder, matmul(centred_full, pre_grad, over_rows))
    return (owned_error, new_encoder, new_decoder)


def solution(mesh):
    cut = Mesh(mesh.devices.reshape(SIZES), AXES)
    return jax.shard_map(
        shards,
        mesh=cut,
        in_specs=(
            P(None, TENSOR),
            P("xl", None, TENSOR),
            P("xl", TENSOR, None),
            P(None, AXES),
            P(AXES),
            P(AXES, None),
            P(),
            P(),
            P(),
        ),
        out_specs=(
            P(TENSOR, "xl"),
            P(None, AXES),
            P(AXES, None),
        ),
        check_vma=False,
    )
```

```python
import jax
import jax.numpy as jnp
from jax import lax
from jax.sharding import Mesh
from jax.sharding import PartitionSpec as P

BOS = 128000


STEP_RATE = 0.5

AXES = ("xl", "y", "zh", "zl", "xh", "c")
SIZES = (2, 4, 4, 2, 2, 2)
NEAR = ("y", "xh", "xl", "zl")
FAR = "zh"
TENSOR = ("y", "zh", "zl", "xh", "c")


def exchange(value, swap):
    route = []
    for source in range(256):
        rest, place = source, {}
        for axis, size in zip(AXES[::-1], SIZES[::-1]):
            place[axis] = rest % size
            rest //= size
        place = swap(place)
        target = 0
        for axis, size in zip(AXES, SIZES):
            target = target * size + place[axis]
        route.append((source, target))
    return lax.ppermute(value, AXES, route)


def other_core(value):
    return exchange(value, lambda p: {**p, "c": 1 - p["c"]})


def core_and_section(value):
    return exchange(value, lambda p: {**p, "c": p["xl"], "xl": p["c"]})


def matmul(a, b, dims=((1,), (0,))):
    return lax.dot_general(a, b, (dims, ((), ())), preferred_element_type=jnp.float32)


def spread(value, axes, count):
    return lax.all_to_all(
        jnp.broadcast_to(value[None], (count,) + value.shape), axes, 0, 0, tiled=True
    )


def near_sum(partial, near):
    tokens, width = partial.shape
    depth = tokens // near
    pieces = lax.all_to_all(partial.reshape(near, depth, width), NEAR, 0, 0, tiled=True)
    to = lax.broadcasted_iota(jnp.int32, (depth, tokens), 0)
    of = lax.broadcasted_iota(jnp.int32, (depth, tokens), 1)
    adds = (of % depth == to).astype(jnp.bfloat16)
    return matmul(adds, pieces.reshape(tokens, width)).astype(jnp.bfloat16)


def far_sum(chunk, far):
    return jnp.sum(spread(chunk, FAR, far).astype(jnp.float32), axis=0)


def shards(
    resid_in, contexts, out_proj, encoder, enc_bias, decoder, dec_bias, token_ids, owner_map
):
    tokens = resid_in.shape[0]
    features = decoder.shape[1]
    own = decoder.shape[0]
    half = features // 2
    blocks = owner_map.shape[0]
    block_rows = tokens // blocks
    far = lax.axis_size(FAR)
    near = blocks // far
    depth = tokens // near
    y, zh, zl, xh, xl, core = (
        lax.axis_index(a) for a in ("y", "zh", "zl", "xh", "xl", "c")
    )

    row = lax.broadcasted_iota(jnp.int32, (tokens, tokens), 0)
    old = lax.broadcasted_iota(jnp.int32, (tokens, tokens), 1)
    slot = row // block_rows
    position = (
        (slot // 32) * 32 + (slot % 4) * 8 + (slot // 4 % 2) * 4 + (slot // 8 % 4)
    )
    owner_of_row = jnp.repeat(owner_map, block_rows)
    order = (
        (owner_of_row[None, :] == position) & (old % block_rows == row % block_rows)
    ).astype(jnp.bfloat16)
    my_slot = ((y * 2 + xh) * 2 + xl) * 2 + zl
    kept = (token_ids != BOS).astype(jnp.bfloat16)
    mask_rows = lax.dynamic_slice_in_dim(
        matmul(order, kept[:, None]), my_slot * depth, depth, 0
    )

    def mine(weight, axis):
        return lax.dynamic_slice_in_dim(weight, core * half, half, axis)

    def theirs(weight, axis):
        return lax.dynamic_slice_in_dim(weight, (1 - core) * half, half, axis)

    proj = out_proj[0]
    proj_other = other_core(theirs(proj, 1))
    width = resid_in.shape[1]
    joined = matmul(order, jnp.concatenate([contexts[0], resid_in], axis=1)).astype(
        jnp.bfloat16
    )
    joined_both = jnp.concatenate([joined, other_core(joined)], axis=1)
    start = (((y * 4 + zh) * 2 + zl) * 2 + xh) * 2 * width
    owns = (start // half == core) & (xl == 0)

    def placed(which):
        column = lax.broadcasted_iota(jnp.int32, (width, half), 1)
        target = lax.broadcasted_iota(jnp.int32, (width, half), 0) + (
            start % half + which * width
        )
        return ((column == target) & owns).astype(jnp.bfloat16)

    proj_both = jnp.concatenate(
        [mine(proj, 1), placed(core), proj_other, placed(1 - core)], axis=0
    )
    partial = matmul(joined_both, proj_both).astype(jnp.bfloat16)

    encoder_late, decoder_late, _ = lax.optimization_barrier((encoder, decoder, partial))
    encoder_both = jnp.concatenate(
        [mine(encoder_late, 0), other_core(theirs(encoder_late, 0))], axis=1
    )
    decoder_both = jnp.concatenate(
        [mine(decoder_late, 1), other_core(theirs(decoder_late, 1))], axis=0
    )
    my_bias = mine(dec_bias, 0).astype(jnp.float32)
    chunk = near_sum(partial, near)
    chunk, encoder_both, decoder_both, mask_rows, my_bias = lax.optimization_barrier(
        (chunk, encoder_both, decoder_both, mask_rows, my_bias)
    )
    values = far_sum(chunk, far).astype(jnp.bfloat16).astype(jnp.float32)
    squares = jnp.sum(values * values, axis=1, keepdims=True)
    squares = squares + other_core(squares)
    inverse_rms = lax.rsqrt(squares / features + 1e-05)
    my_centred = (values * inverse_rms - my_bias).astype(jnp.bfloat16)
    centred = spread(my_centred, NEAR, near).reshape(tokens, half)
    products = matmul(centred, encoder_both)
    before_relu = (
        products[:, :own]
        + other_core(products[:, own:])
        + enc_bias.astype(jnp.float32)
    )
    latents = jnp.maximum(before_relu, 0.0).astype(jnp.bfloat16)
    latents_both = jnp.concatenate([latents, other_core(latents)], axis=1)
    partial = matmul(latents_both, decoder_both).astype(jnp.bfloat16)
    later, _ = lax.optimization_barrier((centred, partial))
    centred_other = other_core(later)
    centred_full = jnp.where(
        core == 0,
        jnp.concatenate([later, centred_other], axis=1),
        jnp.concatenate([centred_other, later], axis=1),
    )
    chunk = near_sum(partial, near)
    chunk, centred_full = lax.optimization_barrier((chunk, centred_full))
    rebuilt = far_sum(chunk, far)
    my_error = (mask_rows * (rebuilt - my_centred.astype(jnp.float32))).astype(jnp.bfloat16)
    error = spread(my_error, NEAR, near).reshape(tokens, half)
    step_size = STEP_RATE / tokens

    def stepped(weight, grad):
        return (weight.astype(jnp.float32) - step_size * grad).astype(jnp.bfloat16)

    over_rows = ((0,), (0,))
    products = matmul(error, decoder_both, ((1,), (1,)))
    backward = products[:, :own] + other_core(products[:, own:])
    pre_grad = lax.optimization_barrier(
        jnp.where(before_relu > 0.0, backward, 0.0).astype(jnp.bfloat16)
    )
    error_late, _ = lax.optimization_barrier((error, products))
    stepped_both = stepped(decoder_both, matmul(latents_both, error_late, over_rows))
    own_rows, _ = lax.optimization_barrier((my_error, products))
    owned_error = core_and_section(
        lax.dynamic_slice_in_dim(own_rows, zh * block_rows, block_rows, 0)
    )
    new_decoder = lax.dynamic_update_slice_in_dim(
        decoder, stepped_both[:own], core * half, 1
    )
    new_decoder = lax.dynamic_update_slice_in_dim(
        new_decoder, other_core(stepped_both[own:]), (1 - core) * half, 1
    )
    new_encoder = stepped(encoder, matmul(centred_full, pre_grad, over_rows))
    return (owned_error, new_encoder, new_decoder)


def solution(mesh):
    cut = Mesh(mesh.devices.reshape(SIZES), AXES)
    return jax.shard_map(
        shards,
        mesh=cut,
        in_specs=(
            P(None, TENSOR),
            P("xl", None, TENSOR),
            P("xl", TENSOR, None),
            P(None, AXES),
            P(AXES),
            P(AXES, None),
            P(),
            P(),
            P(),
        ),
        out_specs=(
            P(TENSOR, "xl"),
            P(None, AXES),
            P(AXES, None),
        ),
        check_vma=False,
    )
```

```python
import jax
import jax.numpy as jnp
from jax import lax
from jax.experimental import pallas as pl
from jax.experimental.pallas import tpu as pltpu
from jax.sharding import Mesh
from jax.sharding import PartitionSpec as P

BOS = 128000


STEP_RATE = 0.5

AXES = ("xl", "y", "z", "xh", "c")
SIZES = (2, 4, 8, 2, 2)
TENSOR = ("y", "z", "xh", "c")
NEAR = 8
FAR = 16


def device(x, y, z, c):
    return (((x % 2 * 4 + y) * 8 + z % 8) * 2 + x // 2) * 2 + c


NEAR_GROUPS = [
    [device(x, y, 2 * w + p, 0) for x in range(4) for p in range(2)]
    for y in range(4)
    for w in range(4)
] + [
    [device(x, y, 2 * w + 1 + p, 1) for y in range(4) for p in range(2)]
    for x in range(4)
    for w in range(4)
]
FAR_GROUPS = [
    [device(x, y, 2 * w + p, 0) for y in range(4) for w in range(4)]
    for x in range(4)
    for p in range(2)
] + [
    [device(x, y, 2 * w + 1 + p, 1) for x in range(4) for w in range(4)]
    for y in range(4)
    for p in range(2)
]


def chip_of(slot, core):
    near, far = slot // FAR, slot % FAR
    line, pair, other, deep = near // 2, near % 2, far // 4, far % 4
    x = jnp.where(core == 0, line, other)
    y = jnp.where(core == 0, other, line)
    z = (2 * deep + pair + core) % 8
    return (y * 8 + z) * 4 + x


def exchange(value, swap):
    route = []
    for xl in range(2):
        for y in range(4):
            for z in range(8):
                for xh in range(2):
                    for c in range(2):
                        xl2, c2 = swap(xl, c)
                        route.append(
                            (device(xh * 2 + xl, y, z, c), device(xh * 2 + xl2, y, z, c2))
                        )
    return lax.ppermute(value, AXES, route)


def other_core(value):
    return exchange(value, lambda xl, c: (xl, 1 - c))


def core_and_section(value):
    return exchange(value, lambda xl, c: (c, xl))


def matmul(a, b, dims=((1,), (0,)), **how):
    return lax.dot_general(
        a, b, (dims, ((), ())), preferred_element_type=jnp.float32, **how
    )


def all_to_all(pieces, groups):
    return lax.all_to_all(pieces, AXES, 0, 0, axis_index_groups=groups, tiled=True)


def spread(value, groups, count):
    stacked = jnp.broadcast_to(value[None], (count,) + value.shape)
    return all_to_all(stacked, groups).reshape(-1, value.shape[1])


def near_sum(partial):
    tokens, width = partial.shape
    depth = tokens // NEAR
    pieces = all_to_all(partial.reshape(NEAR, depth, width), NEAR_GROUPS)
    to = lax.broadcasted_iota(jnp.int32, (depth, tokens), 0)
    of = lax.broadcasted_iota(jnp.int32, (depth, tokens), 1)
    adds = (of % depth == to).astype(jnp.bfloat16)
    return matmul(adds, pieces.reshape(tokens, width)).astype(jnp.bfloat16)


def far_sum(chunk):
    pieces = all_to_all(chunk.reshape(FAR, -1, chunk.shape[1]), FAR_GROUPS)
    return jnp.sum(pieces.astype(jnp.float32), axis=0)


def place(core_ref, kept_ref, back_ref, out_ref, sems):
    half = kept_ref.shape[1]
    core = core_ref[0]
    copies = [
        pltpu.make_async_copy(
            ref, out_ref.at[:, pl.ds(pl.multiple_of(at * half, half), half)], sems.at[i]
        )
        for i, (ref, at) in enumerate(((kept_ref, core), (back_ref, 1 - core)))
    ]
    for copy in copies:
        copy.start()
    for copy in copies:
        copy.wait()


def join_columns(core, kept, back):
    rows, half = kept.shape
    return pl.pallas_call(
        place,
        grid_spec=pltpu.PrefetchScalarGridSpec(
            num_scalar_prefetch=1,
            grid=(1,),
            in_specs=[pl.BlockSpec(memory_space=pl.ANY)] * 2,
            out_specs=pl.BlockSpec(memory_space=pl.ANY),
            scratch_shapes=[pltpu.SemaphoreType.DMA((2,))],
        ),
        out_shape=jax.ShapeDtypeStruct((rows, 2 * half), kept.dtype),
        cost_estimate=pl.CostEstimate(
            flops=0, bytes_accessed=8 * rows * half, transcendentals=0
        ),
    )(jnp.reshape(core, (1,)).astype(jnp.int32), kept, back)


def shards(
    resid_in, contexts, out_proj, encoder, enc_bias, decoder, dec_bias, token_ids, owner_map
):
    tokens, width = resid_in.shape
    own, features = decoder.shape
    half = features // 2
    blocks = owner_map.shape[0]
    block_rows = tokens // blocks
    y, z, xh, xl, core = (lax.axis_index(a) for a in ("y", "z", "xh", "xl", "c"))
    chip = (y * 8 + z) * 4 + xh * 2 + xl

    def mine(weight, axis):
        return lax.dynamic_slice_in_dim(weight, core * half, half, axis)

    def theirs(weight, axis):
        return lax.dynamic_slice_in_dim(weight, (1 - core) * half, half, axis)

    proj = out_proj[0]
    proj_other = other_core(theirs(proj, 1))
    context_other = other_core(contexts[0])
    resid_other = other_core(resid_in)

    row = lax.broadcasted_iota(jnp.int32, (tokens, tokens), 0)
    old = lax.broadcasted_iota(jnp.int32, (tokens, tokens), 1)
    same_place = row % block_rows == old % block_rows
    at = chip_of(row // block_rows, core)
    owner_of_row = jnp.repeat(owner_map, block_rows)
    order = ((owner_of_row[None, :] == at) & same_place).astype(jnp.bfloat16)
    across = (chip_of(old // block_rows, 1 - core) == at) & same_place
    kept = (token_ids.reshape(blocks, block_rows) != BOS).astype(jnp.float32)
    mask_rows = jnp.sum(jnp.where((owner_map == chip)[:, None], kept, 0.0), axis=0)[:, None]

    start = ((y * 8 + z) * 2 + xh) * 2 * width
    owns = (start // half == core) & (xl == 0)

    def placed(which):
        column = lax.broadcasted_iota(jnp.int32, (width, half), 1)
        target = lax.broadcasted_iota(jnp.int32, (width, half), 0) + (
            start % half + which * width
        )
        return ((column == target) & owns).astype(jnp.bfloat16)

    joined = matmul(
        order,
        jnp.concatenate([contexts[0], context_other, resid_in, resid_other], axis=1),
    ).astype(jnp.bfloat16)
    proj_both = jnp.concatenate(
        [mine(proj, 1), proj_other, placed(core), placed(1 - core)], axis=0
    )
    partial = matmul(joined, proj_both).astype(jnp.bfloat16)

    encoder_out, decoder_out, _ = lax.optimization_barrier(
        (theirs(encoder, 0), theirs(decoder, 1), partial)
    )
    encoder_own, encoder_other = mine(encoder, 0), other_core(encoder_out)
    decoder_both = jnp.concatenate([mine(decoder, 1), other_core(decoder_out)], axis=0)
    my_bias = mine(dec_bias, 0).astype(jnp.float32)
    chunk = near_sum(partial)
    chunk, encoder_own, encoder_other, decoder_both, mask_rows, my_bias, across = (
        lax.optimization_barrier(
            (chunk, encoder_own, encoder_other, decoder_both, mask_rows, my_bias, across)
        )
    )
    values = far_sum(chunk).astype(jnp.bfloat16).astype(jnp.float32)
    squares = jnp.sum(values * values, axis=1, keepdims=True)
    squares = squares + other_core(squares)
    inverse_rms = lax.rsqrt(squares / features + 1e-05)
    my_centred = (values * inverse_rms - my_bias).astype(jnp.bfloat16)
    centred = spread(spread(my_centred, FAR_GROUPS, FAR), NEAR_GROUPS, NEAR)

    exact = dict(precision=lax.Precision.HIGHEST)

    def both_halves(own_weight, other_weight, values, dims):
        sent = other_core(matmul(other_weight, values, dims))
        kept = matmul(own_weight, values, dims)
        return kept + matmul(sent, across.astype(jnp.float32), ((1,), (1,)), **exact)

    before_relu = both_halves(encoder_own, encoder_other, centred, ((0,), (1,)))
    before_relu = before_relu + enc_bias.astype(jnp.float32)[:, None]
    latents = jnp.maximum(before_relu, 0.0).astype(jnp.bfloat16)
    across_low = across.astype(jnp.bfloat16)
    latents_other = matmul(other_core(latents), across_low, ((1,), (1,))).astype(jnp.bfloat16)
    latents_both = jnp.concatenate([latents, latents_other], axis=0)
    partial = matmul(latents_both, decoder_both, ((0,), (0,))).astype(jnp.bfloat16)
    later, _ = lax.optimization_barrier((centred, partial))
    centred_other = matmul(
        other_core(later), across_low, ((0,), (1,))
    ).astype(jnp.bfloat16)
    centred_own = later.T
    centred_full = jnp.where(
        core == 0,
        jnp.concatenate([centred_own, centred_other], axis=0),
        jnp.concatenate([centred_other, centred_own], axis=0),
    )
    chunk = near_sum(partial)
    chunk, centred_full = lax.optimization_barrier((chunk, centred_full))
    rebuilt = far_sum(chunk)
    my_error = (mask_rows * (rebuilt - my_centred.astype(jnp.float32))).astype(jnp.bfloat16)
    owned_error = core_and_section(my_error)
    error = spread(spread(my_error, FAR_GROUPS, FAR), NEAR_GROUPS, NEAR)
    step_size = STEP_RATE / tokens

    def stepped(weight, grad):
        return (weight.astype(jnp.float32) - step_size * grad).astype(jnp.bfloat16)

    decoder_own, decoder_other = decoder_both[:own], decoder_both[own:]
    backward = both_halves(decoder_own, decoder_other, error, ((1,), (1,)))
    pre_grad = lax.optimization_barrier(
        jnp.where(before_relu > 0.0, backward, 0.0).astype(jnp.bfloat16)
    )
    back = other_core(stepped(decoder_other, matmul(latents_other, error)))
    new_decoder = join_columns(core, stepped(decoder_own, matmul(latents, error)), back)
    new_encoder = stepped(encoder, matmul(centred_full, pre_grad, ((1,), (1,))))
    return (owned_error, new_encoder, new_decoder)


def solution(mesh):
    cut = Mesh(mesh.devices.reshape(SIZES), AXES)
    return jax.shard_map(
        shards,
        mesh=cut,
        in_specs=(
            P(None, TENSOR),
            P("xl", None, TENSOR),
            P("xl", TENSOR, None),
            P(None, AXES),
            P(AXES),
            P(AXES, None),
            P(),
            P(),
            P(),
        ),
        out_specs=(
            P(TENSOR, "xl"),
            P(None, AXES),
            P(AXES, None),
        ),
        check_vma=False,
    )
```

```python
import jax
import jax.numpy as jnp
from jax import lax
from jax.experimental import pallas as pl
from jax.experimental.pallas import tpu as pltpu
from jax.sharding import Mesh
from jax.sharding import PartitionSpec as P

BOS = 128000


STEP_RATE = 0.5

AXES = ("xl", "y", "z", "xh", "c")
SIZES = (2, 4, 8, 2, 2)
TENSOR = ("y", "z", "xh", "c")
NEAR = 8
FAR = 16


def device(x, y, z, c):
    return (((x % 2 * 4 + y) * 8 + z % 8) * 2 + x // 2) * 2 + c


NEAR_GROUPS = [
    [device(x, y, 2 * w + p, 0) for x in range(4) for p in range(2)]
    for y in range(4)
    for w in range(4)
] + [
    [device(x, y, 2 * w + 1 + p, 1) for y in range(4) for p in range(2)]
    for x in range(4)
    for w in range(4)
]
FAR_GROUPS = [
    [device(x, y, 2 * w + p, 0) for y in range(4) for w in range(4)]
    for x in range(4)
    for p in range(2)
] + [
    [device(x, y, 2 * w + 1 + p, 1) for x in range(4) for w in range(4)]
    for y in range(4)
    for p in range(2)
]


def chip_of(slot, core):
    near, far = slot // FAR, slot % FAR
    line, pair, other, deep = near // 2, near % 2, far // 4, far % 4
    x = jnp.where(core == 0, line, other)
    y = jnp.where(core == 0, other, line)
    z = (2 * deep + pair + core) % 8
    return (y * 8 + z) * 4 + x


def exchange(value, swap):
    route = []
    for xl in range(2):
        for y in range(4):
            for z in range(8):
                for xh in range(2):
                    for c in range(2):
                        xl2, c2 = swap(xl, c)
                        route.append(
                            (device(xh * 2 + xl, y, z, c), device(xh * 2 + xl2, y, z, c2))
                        )
    return lax.ppermute(value, AXES, route)


def other_core(value):
    return exchange(value, lambda xl, c: (xl, 1 - c))


def core_and_section(value):
    return exchange(value, lambda xl, c: (c, xl))


def matmul(a, b, dims=((1,), (0,)), **how):
    return lax.dot_general(
        a, b, (dims, ((), ())), preferred_element_type=jnp.float32, **how
    )


def all_to_all(pieces, groups):
    return lax.all_to_all(pieces, AXES, 0, 0, axis_index_groups=groups, tiled=True)


def spread(value, groups, count):
    stacked = jnp.broadcast_to(value[None], (count,) + value.shape)
    return all_to_all(stacked, groups).reshape(-1, value.shape[1])


def near_sum(partial):
    tokens, width = partial.shape
    depth = tokens // NEAR
    pieces = all_to_all(partial.reshape(NEAR, depth, width), NEAR_GROUPS)
    to = lax.broadcasted_iota(jnp.int32, (depth, tokens), 0)
    of = lax.broadcasted_iota(jnp.int32, (depth, tokens), 1)
    adds = (of % depth == to).astype(jnp.bfloat16)
    return matmul(adds, pieces.reshape(tokens, width)).astype(jnp.bfloat16)


def far_sum(chunk):
    pieces = all_to_all(chunk.reshape(FAR, -1, chunk.shape[1]), FAR_GROUPS)
    return jnp.sum(pieces.astype(jnp.float32), axis=0)


def project(
    at_ref, order_ref, context_ref, context2_ref, resid_ref, resid2_ref, own_ref, other_ref,
    out_ref, context_rows, context2_rows, resid_rows, resid2_rows,
):
    tile = pl.program_id(0)

    @pl.when(tile == 0)
    def _():
        for source, rows in (
            (context_ref, context_rows),
            (context2_ref, context2_rows),
            (resid_ref, resid_rows),
            (resid2_ref, resid2_rows),
        ):
            rows[...] = matmul(order_ref[...], source[...]).astype(jnp.bfloat16)

    width, columns = resid_ref.shape[1], out_ref.shape[1]
    shift = lax.broadcasted_iota(jnp.int32, (width, columns), 1) - lax.broadcasted_iota(
        jnp.int32, (width, columns), 0
    )
    total = matmul(context_rows[...], own_ref[...]) + matmul(context2_rows[...], other_ref[...])
    for rows, which in ((resid_rows, 0), (resid2_rows, 1)):
        placed = jnp.where(shift == at_ref[1 + which] - tile * columns, 1.0, 0.0)
        total += matmul(rows[...], placed.astype(jnp.bfloat16))
    out_ref[...] = total.astype(jnp.bfloat16)


def project_both(at, order, context, context2, resid, resid2, proj, proj_other):
    tokens, depth = context.shape
    half = proj_other.shape[1]
    columns = half // 8
    whole = lambda array: pl.BlockSpec(array.shape, lambda j, at: (0, 0))
    return pl.pallas_call(
        project,
        grid_spec=pltpu.PrefetchScalarGridSpec(
            num_scalar_prefetch=1,
            grid=(8,),
            in_specs=[
                whole(order),
                whole(context),
                whole(context2),
                whole(resid),
                whole(resid2),
                pl.BlockSpec((depth, columns), lambda j, at: (0, at[0] * 8 + j)),
                pl.BlockSpec((depth, columns), lambda j, at: (0, j)),
            ],
            out_specs=pl.BlockSpec((tokens, columns), lambda j, at: (0, j)),
            scratch_shapes=[
                pltpu.VMEM(array.shape, jnp.bfloat16)
                for array in (context, context2, resid, resid2)
            ],
        ),
        out_shape=jax.ShapeDtypeStruct((tokens, half), jnp.bfloat16),
        cost_estimate=pl.CostEstimate(
            flops=6 * tokens * depth * half,
            bytes_accessed=4 * half * (depth + tokens // 2),
            transcendentals=0,
        ),
    )(at, order, context, context2, resid, resid2, proj, proj_other)


def products(dims, core_ref, rows_ref, own_ref, other_ref, to_other_ref, kept_ref, sent_ref):
    tile = pl.program_id(0)

    @pl.when(tile == 0)
    def _():
        kept_ref[...] = jnp.zeros_like(kept_ref)
        sent_ref[...] = jnp.zeros_like(sent_ref)

    kept_ref[...] += matmul(rows_ref[...], own_ref[...], dims)
    sent_ref[...] += matmul(rows_ref[...], other_ref[...], dims)

    @pl.when(tile == pl.num_programs(0) - 1)
    def _():
        sent_ref[...] = matmul(
            to_other_ref[...], sent_ref[...], precision=lax.Precision.HIGHEST
        )


def both_products(core, rows, weight, other, to_other, along):
    tokens, half = rows.shape
    own = weight.shape[1 - along]
    steps = 4
    tile = half // steps
    shape = (tile, own) if along == 0 else (own, tile)
    spot = lambda at: (at, 0) if along == 0 else (0, at)
    result = jax.ShapeDtypeStruct((tokens, own), jnp.float32)
    return pl.pallas_call(
        lambda *refs: products(((1,), (along,)), *refs),
        grid_spec=pltpu.PrefetchScalarGridSpec(
            num_scalar_prefetch=1,
            grid=(steps,),
            in_specs=[
                pl.BlockSpec((tokens, tile), lambda k, core: (0, k)),
                pl.BlockSpec(shape, lambda k, core: spot(core[0] * steps + k)),
                pl.BlockSpec(shape, lambda k, core: spot(k)),
                pl.BlockSpec((tokens, tokens), lambda k, core: (0, 0)),
            ],
            out_specs=[pl.BlockSpec((tokens, own), lambda k, core: (0, 0))] * 2,
        ),
        out_shape=[result, result],
        cost_estimate=pl.CostEstimate(
            flops=4 * tokens * half * own,
            bytes_accessed=2 * half * (tokens + 2 * own),
            transcendentals=0,
        ),
    )(core, rows, weight, other, to_other)


def shards(
    resid_in, contexts, out_proj, encoder, enc_bias, decoder, dec_bias, token_ids, owner_map
):
    tokens, width = resid_in.shape
    own, features = decoder.shape
    half = features // 2
    blocks = owner_map.shape[0]
    block_rows = tokens // blocks
    y, z, xh, xl, core = (lax.axis_index(a) for a in ("y", "z", "xh", "xl", "c"))
    chip = (y * 8 + z) * 4 + xh * 2 + xl

    def mine(weight, axis):
        return lax.dynamic_slice_in_dim(weight, core * half, half, axis)

    def theirs(weight, axis):
        return lax.dynamic_slice_in_dim(weight, (1 - core) * half, half, axis)

    proj = out_proj[0]
    proj_other = other_core(theirs(proj, 1))
    context_other = other_core(contexts[0])
    resid_other = other_core(resid_in)

    row = lax.broadcasted_iota(jnp.int32, (tokens, tokens), 0)
    old = lax.broadcasted_iota(jnp.int32, (tokens, tokens), 1)
    same_place = row % block_rows == old % block_rows
    at = chip_of(row // block_rows, core)
    owner_of_row = jnp.repeat(owner_map, block_rows)
    order = ((owner_of_row[None, :] == at) & same_place).astype(jnp.bfloat16)
    across = ((chip_of(old // block_rows, 1 - core) == at) & same_place).astype(jnp.bfloat16)
    to_other = (
        (chip_of(row // block_rows, 1 - core) == chip_of(old // block_rows, core)) & same_place
    ).astype(jnp.float32)
    kept = (token_ids.reshape(blocks, block_rows) != BOS).astype(jnp.float32)
    mask_rows = jnp.sum(jnp.where((owner_map == chip)[:, None], kept, 0.0), axis=0)[:, None]

    start = ((y * 8 + z) * 2 + xh) * 2 * width
    owns = (start // half == core) & (xl == 0)
    start = jnp.where(owns, start % half, -features)
    core_at = jnp.reshape(core, (1,)).astype(jnp.int32)
    places = jnp.stack([core, start + core * width, start + (1 - core) * width]).astype(jnp.int32)
    partial = project_both(
        places, order, contexts[0], context_other, resid_in, resid_other, proj, proj_other
    )

    encoder_out, decoder_out, _ = lax.optimization_barrier(
        (theirs(encoder, 0), theirs(decoder, 1), partial)
    )
    encoder_other, decoder_other = other_core(encoder_out), other_core(decoder_out)
    decoder_both = jnp.concatenate([mine(decoder, 1), decoder_other], axis=0)
    my_bias = mine(dec_bias, 0).astype(jnp.float32)
    chunk = near_sum(partial)
    chunk, encoder_other, decoder_other, decoder_both, mask_rows, my_bias, across, to_other = (
        lax.optimization_barrier(
            (
                chunk,
                encoder_other,
                decoder_other,
                decoder_both,
                mask_rows,
                my_bias,
                across,
                to_other,
            )
        )
    )
    values = far_sum(chunk).astype(jnp.bfloat16).astype(jnp.float32)
    squares = jnp.sum(values * values, axis=1, keepdims=True)
    squares = squares + other_core(squares)
    inverse_rms = lax.rsqrt(squares / features + 1e-05)
    my_centred = (values * inverse_rms - my_bias).astype(jnp.bfloat16)
    centred = spread(spread(my_centred, FAR_GROUPS, FAR), NEAR_GROUPS, NEAR)

    products_own, products_sent = both_products(
        core_at, centred, encoder, encoder_other, to_other, 0
    )
    before_relu = products_own + other_core(products_sent) + enc_bias.astype(jnp.float32)
    latents = jnp.maximum(before_relu, 0.0).astype(jnp.bfloat16)
    latents_other = other_core(
        matmul(to_other.astype(jnp.bfloat16), latents).astype(jnp.bfloat16)
    )
    latents_both = jnp.concatenate([latents, latents_other], axis=1)
    partial = matmul(latents_both, decoder_both).astype(jnp.bfloat16)
    later, _ = lax.optimization_barrier((centred, partial))
    centred_other = matmul(
        other_core(later), across, ((0,), (1,))
    ).astype(jnp.bfloat16)
    centred_own = later.T
    centred_full = jnp.where(
        core == 0,
        jnp.concatenate([centred_own, centred_other], axis=0),
        jnp.concatenate([centred_other, centred_own], axis=0),
    )
    chunk = near_sum(partial)
    chunk, centred_full = lax.optimization_barrier((chunk, centred_full))
    rebuilt = far_sum(chunk)
    my_error = (mask_rows * (rebuilt - my_centred.astype(jnp.float32))).astype(jnp.bfloat16)
    owned_error = core_and_section(my_error)
    error = spread(spread(my_error, FAR_GROUPS, FAR), NEAR_GROUPS, NEAR)
    step_size = STEP_RATE / tokens

    def stepped(weight, grad):
        return (weight.astype(jnp.float32) - step_size * grad).astype(jnp.bfloat16)

    products_own, products_sent = both_products(
        core_at, error, decoder, decoder_other, to_other, 1
    )
    backward = products_own + other_core(products_sent)
    pre_grad = lax.optimization_barrier(
        jnp.where(before_relu > 0.0, backward, 0.0).astype(jnp.bfloat16)
    )
    over_rows = ((0,), (0,))
    error_late, _ = lax.optimization_barrier((error, products_sent))
    back = other_core(stepped(decoder_other, matmul(latents_other, error_late, over_rows)))
    kept_half = stepped(decoder_both[:own], matmul(latents, error_late, over_rows))
    new_encoder = stepped(encoder, matmul(centred_full, pre_grad))
    new_decoder = jnp.where(
        core == 0,
        jnp.concatenate([kept_half, back], axis=1),
        jnp.concatenate([back, kept_half], axis=1),
    )
    return (owned_error, new_encoder, new_decoder)


def solution(mesh):
    cut = Mesh(mesh.devices.reshape(SIZES), AXES)
    return jax.shard_map(
        shards,
        mesh=cut,
        in_specs=(
            P(None, TENSOR),
            P("xl", None, TENSOR),
            P("xl", TENSOR, None),
            P(None, AXES),
            P(AXES),
            P(AXES, None),
            P(),
            P(),
            P(),
        ),
        out_specs=(
            P(TENSOR, "xl"),
            P(None, AXES),
            P(AXES, None),
        ),
        check_vma=False,
    )
```

```python
import jax
import jax.numpy as jnp
from jax import lax
from jax.sharding import Mesh
from jax.sharding import PartitionSpec as P

BOS = 128000


STEP_RATE = 0.5

AXES = ("xl", "y", "z", "xh", "c")
SIZES = (2, 4, 8, 2, 2)
TENSOR = ("y", "z", "xh", "c")
NEAR = 8
FAR = 16


def device(x, y, z, c):
    return (((x % 2 * 4 + y) * 8 + z % 8) * 2 + x // 2) * 2 + c


NEAR_GROUPS = [
    [device(x, y, 2 * w + p, 0) for x in range(4) for p in range(2)]
    for y in range(4)
    for w in range(4)
] + [
    [device(x, y, 2 * w + 1 + p, 1) for y in range(4) for p in range(2)]
    for x in range(4)
    for w in range(4)
]
FAR_GROUPS = [
    [device(x, y, 2 * w + p, 0) for y in range(4) for w in range(4)]
    for x in range(4)
    for p in range(2)
] + [
    [device(x, y, 2 * w + 1 + p, 1) for x in range(4) for w in range(4)]
    for y in range(4)
    for p in range(2)
]


def chip_of(slot, core):
    near, far = slot // FAR, slot % FAR
    line, pair, other, deep = near // 2, near % 2, far // 4, far % 4
    x = jnp.where(core == 0, line, other)
    y = jnp.where(core == 0, other, line)
    z = (2 * deep + pair + core) % 8
    return (y * 8 + z) * 4 + x


def exchange(value, swap):
    route = []
    for xl in range(2):
        for y in range(4):
            for z in range(8):
                for xh in range(2):
                    for c in range(2):
                        xl2, c2 = swap(xl, c)
                        route.append(
                            (device(xh * 2 + xl, y, z, c), device(xh * 2 + xl2, y, z, c2))
                        )
    return lax.ppermute(value, AXES, route)


def other_core(value):
    return exchange(value, lambda xl, c: (xl, 1 - c))


def core_and_section(value):
    return exchange(value, lambda xl, c: (c, xl))


def matmul(a, b, dims=((1,), (0,)), **how):
    return lax.dot_general(
        a, b, (dims, ((), ())), preferred_element_type=jnp.float32, **how
    )


def all_to_all(pieces, groups):
    return lax.all_to_all(pieces, AXES, 0, 0, axis_index_groups=groups, tiled=True)


def spread(value, groups, count):
    stacked = jnp.broadcast_to(value[None], (count,) + value.shape)
    return all_to_all(stacked, groups).reshape(-1, value.shape[1])


def near_sum(partial):
    tokens, width = partial.shape
    depth = tokens // NEAR
    pieces = all_to_all(partial.reshape(NEAR, depth, width), NEAR_GROUPS)
    to = lax.broadcasted_iota(jnp.int32, (depth, tokens), 0)
    of = lax.broadcasted_iota(jnp.int32, (depth, tokens), 1)
    adds = (of % depth == to).astype(jnp.bfloat16)
    return matmul(adds, pieces.reshape(tokens, width)).astype(jnp.bfloat16)


def far_sum(chunk):
    pieces = all_to_all(chunk.reshape(FAR, -1, chunk.shape[1]), FAR_GROUPS)
    return jnp.sum(pieces.astype(jnp.float32), axis=0)


def shards(
    resid_in, contexts, out_proj, encoder, enc_bias, decoder, dec_bias, token_ids, owner_map
):
    tokens, width = resid_in.shape
    own, features = decoder.shape
    half = features // 2
    blocks = owner_map.shape[0]
    block_rows = tokens // blocks
    y, z, xh, xl, core = (lax.axis_index(a) for a in ("y", "z", "xh", "xl", "c"))
    chip = (y * 8 + z) * 4 + xh * 2 + xl

    def mine(weight, axis):
        return lax.dynamic_slice_in_dim(weight, core * half, half, axis)

    def theirs(weight, axis):
        return lax.dynamic_slice_in_dim(weight, (1 - core) * half, half, axis)

    proj = out_proj[0]
    proj_other = other_core(theirs(proj, 1))
    context_other = other_core(contexts[0])
    resid_other = other_core(resid_in)

    row = lax.broadcasted_iota(jnp.int32, (tokens, tokens), 0)
    old = lax.broadcasted_iota(jnp.int32, (tokens, tokens), 1)
    same_place = row % block_rows == old % block_rows
    at = chip_of(row // block_rows, core)
    owner_of_row = jnp.repeat(owner_map, block_rows)
    order = ((owner_of_row[None, :] == at) & same_place).astype(jnp.bfloat16)
    across = (chip_of(old // block_rows, 1 - core) == at) & same_place
    kept = (token_ids.reshape(blocks, block_rows) != BOS).astype(jnp.float32)
    mask_rows = jnp.sum(jnp.where((owner_map == chip)[:, None], kept, 0.0), axis=0)[:, None]

    start = ((y * 8 + z) * 2 + xh) * 2 * width
    owns = (start // half == core) & (xl == 0)

    def placed(which):
        column = lax.broadcasted_iota(jnp.int32, (width, half), 1)
        target = lax.broadcasted_iota(jnp.int32, (width, half), 0) + (
            start % half + which * width
        )
        return ((column == target) & owns).astype(jnp.bfloat16)

    joined = matmul(
        order,
        jnp.concatenate([contexts[0], context_other, resid_in, resid_other], axis=1),
    ).astype(jnp.bfloat16)
    joined = lax.optimization_barrier(joined)
    proj_both = jnp.concatenate(
        [mine(proj, 1), proj_other, placed(core), placed(1 - core)], axis=0
    )
    partial = matmul(joined, proj_both).astype(jnp.bfloat16)

    encoder_out, decoder_out, _ = lax.optimization_barrier(
        (theirs(encoder, 0), theirs(decoder, 1), partial)
    )
    encoder_both = jnp.concatenate([mine(encoder, 0), other_core(encoder_out)], axis=1)
    decoder_both = jnp.concatenate([mine(decoder, 1), other_core(decoder_out)], axis=0)
    my_bias = mine(dec_bias, 0).astype(jnp.float32)
    chunk = near_sum(partial)
    chunk, encoder_both, decoder_both, mask_rows, my_bias, across = lax.optimization_barrier(
        (chunk, encoder_both, decoder_both, mask_rows, my_bias, across)
    )
    values = far_sum(chunk).astype(jnp.bfloat16).astype(jnp.float32)
    squares = jnp.sum(values * values, axis=1, keepdims=True)
    squares = squares + other_core(squares)
    inverse_rms = lax.rsqrt(squares / features + 1e-05)
    my_centred = (values * inverse_rms - my_bias).astype(jnp.bfloat16)
    centred = spread(spread(my_centred, FAR_GROUPS, FAR), NEAR_GROUPS, NEAR)

    exact = dict(precision=lax.Precision.HIGHEST)

    def in_my_order(arrived):
        return matmul(arrived, across.astype(jnp.float32), ((1,), (1,)), **exact)

    products = matmul(centred, encoder_both).T
    before_relu = products[:own] + in_my_order(other_core(products[own:]))
    before_relu = before_relu + enc_bias.astype(jnp.float32)[:, None]
    latents = jnp.maximum(before_relu, 0.0).astype(jnp.bfloat16)
    across_low = across.astype(jnp.bfloat16)
    latents_other = matmul(other_core(latents), across_low, ((1,), (1,))).astype(jnp.bfloat16)
    latents_both = jnp.concatenate([latents, latents_other], axis=0)
    partial = matmul(latents_both, decoder_both, ((0,), (0,))).astype(jnp.bfloat16)
    later, _ = lax.optimization_barrier((centred, partial))
    centred_other = matmul(
        other_core(later), across_low, ((0,), (1,))
    ).astype(jnp.bfloat16)
    centred_own = later.T
    centred_full = jnp.where(
        core == 0,
        jnp.concatenate([centred_own, centred_other], axis=0),
        jnp.concatenate([centred_other, centred_own], axis=0),
    )
    chunk = near_sum(partial)
    chunk, centred_full = lax.optimization_barrier((chunk, centred_full))
    rebuilt = far_sum(chunk)
    my_error = (mask_rows * (rebuilt - my_centred.astype(jnp.float32))).astype(jnp.bfloat16)
    owned_error = core_and_section(my_error)
    error = spread(spread(my_error, FAR_GROUPS, FAR), NEAR_GROUPS, NEAR)
    step_size = STEP_RATE / tokens

    def stepped(weight, grad):
        return (weight.astype(jnp.float32) - step_size * grad).astype(jnp.bfloat16)

    decoder_own, decoder_other = decoder_both[:own], decoder_both[own:]
    over_features = ((1,), (1,))
    arrived = other_core(matmul(decoder_other, error, over_features))
    backward = matmul(decoder_own, error, over_features) + in_my_order(arrived)
    pre_grad = lax.optimization_barrier(
        jnp.where(before_relu > 0.0, backward, 0.0).astype(jnp.bfloat16)
    )
    back_half = other_core(stepped(decoder_other, matmul(latents_other, error)))
    kept_half = stepped(decoder_own, matmul(latents, error))
    new_encoder = stepped(encoder, matmul(centred_full, pre_grad, over_features))
    new_decoder = jnp.where(
        core == 0,
        jnp.concatenate([kept_half, back_half], axis=1),
        jnp.concatenate([back_half, kept_half], axis=1),
    )
    return (owned_error, new_encoder, new_decoder)


def solution(mesh):
    cut = Mesh(mesh.devices.reshape(SIZES), AXES)
    return jax.shard_map(
        shards,
        mesh=cut,
        in_specs=(
            P(None, TENSOR),
            P("xl", None, TENSOR),
            P("xl", TENSOR, None),
            P(None, AXES),
            P(AXES),
            P(AXES, None),
            P(),
            P(),
            P(),
        ),
        out_specs=(
            P(TENSOR, "xl"),
            P(None, AXES),
            P(AXES, None),
        ),
        check_vma=False,
    )
```

```python
import jax
import jax.numpy as jnp
from jax import lax
from jax.sharding import Mesh
from jax.sharding import PartitionSpec as P

BOS = 128000


STEP_RATE = 0.5

AXES = ("xl", "y", "z", "xh", "c")
SIZES = (2, 4, 8, 2, 2)
TENSOR = ("y", "z", "xh", "c")
NEAR = 8
FAR = 16


def device(x, y, z, c):
    return (((x % 2 * 4 + y) * 8 + z % 8) * 2 + x // 2) * 2 + c


NEAR_GROUPS = [
    [device(x, y, 2 * w + p, 0) for x in range(4) for p in range(2)]
    for y in range(4)
    for w in range(4)
] + [
    [device(x, y, 2 * w + 1 + p, 1) for y in range(4) for p in range(2)]
    for x in range(4)
    for w in range(4)
]
FAR_GROUPS = [
    [device(x, y, 2 * w + p, 0) for y in range(4) for w in range(4)]
    for x in range(4)
    for p in range(2)
] + [
    [device(x, y, 2 * w + 1 + p, 1) for x in range(4) for w in range(4)]
    for y in range(4)
    for p in range(2)
]


def chip_of(slot, core):
    near, far = slot // FAR, slot % FAR
    line, pair, other, deep = near // 2, near % 2, far // 4, far % 4
    x = jnp.where(core == 0, line, other)
    y = jnp.where(core == 0, other, line)
    z = (2 * deep + pair + core) % 8
    return (y * 8 + z) * 4 + x


def exchange(value, swap):
    route = []
    for xl in range(2):
        for y in range(4):
            for z in range(8):
                for xh in range(2):
                    for c in range(2):
                        xl2, c2 = swap(xl, c)
                        route.append(
                            (device(xh * 2 + xl, y, z, c), device(xh * 2 + xl2, y, z, c2))
                        )
    return lax.ppermute(value, AXES, route)


def other_core(value):
    return exchange(value, lambda xl, c: (xl, 1 - c))


def core_and_section(value):
    return exchange(value, lambda xl, c: (c, xl))


def matmul(a, b, dims=((1,), (0,)), **how):
    return lax.dot_general(
        a, b, (dims, ((), ())), preferred_element_type=jnp.float32, **how
    )


def all_to_all(pieces, groups):
    return lax.all_to_all(pieces, AXES, 0, 0, axis_index_groups=groups, tiled=True)


def spread(value, groups, count):
    stacked = jnp.broadcast_to(value[None], (count,) + value.shape)
    return all_to_all(stacked, groups).reshape(-1, value.shape[1])


def near_sum(partial, adds):
    tokens, width = partial.shape
    pieces = all_to_all(partial.reshape(NEAR, tokens // NEAR, width), NEAR_GROUPS)
    return matmul(adds, pieces.reshape(tokens, width)).astype(jnp.bfloat16)


def far_sum(chunk):
    pieces = all_to_all(chunk.reshape(FAR, -1, chunk.shape[1]), FAR_GROUPS)
    return jnp.sum(pieces.astype(jnp.float32), axis=0)


def shards(
    resid_in, contexts, out_proj, encoder, enc_bias, decoder, dec_bias, token_ids, owner_map
):
    tokens, width = resid_in.shape
    own, features = decoder.shape
    half = features // 2
    blocks = owner_map.shape[0]
    block_rows = tokens // blocks
    y, z, xh, xl, core = (lax.axis_index(a) for a in ("y", "z", "xh", "xl", "c"))
    chip = (y * 8 + z) * 4 + xh * 2 + xl

    def mine(weight, axis, core):
        return lax.dynamic_slice_in_dim(weight, core * half, half, axis)

    def theirs(weight, axis, core):
        return lax.dynamic_slice_in_dim(weight, (1 - core) * half, half, axis)

    proj = out_proj[0]
    proj_out, resid, context, core_head = lax.optimization_barrier(
        (theirs(proj, 1, core), resid_in, contexts[0], core)
    )
    proj_other = other_core(proj_out)
    context_other = other_core(context)
    resid_other = other_core(resid)

    row = lax.broadcasted_iota(jnp.int32, (tokens, tokens), 0)
    old = lax.broadcasted_iota(jnp.int32, (tokens, tokens), 1)
    same_place = row % block_rows == old % block_rows
    at = chip_of(row // block_rows, core)
    owner_of_row = jnp.repeat(owner_map, block_rows)
    order = ((owner_of_row[None, :] == at) & same_place).astype(jnp.bfloat16)

    start = ((y * 8 + z) * 2 + xh) * 2 * width
    owns = (start // half == core) & (xl == 0)

    def placed(which):
        column = lax.broadcasted_iota(jnp.int32, (width, half), 1)
        target = lax.broadcasted_iota(jnp.int32, (width, half), 0) + (
            start % half + which * width
        )
        return ((column == target) & owns).astype(jnp.bfloat16)

    depth = tokens // NEAR
    to = lax.broadcasted_iota(jnp.int32, (depth, tokens), 0)
    of = lax.broadcasted_iota(jnp.int32, (depth, tokens), 1)
    joined = matmul(
        order, jnp.concatenate([context, context_other, resid, resid_other], axis=1)
    ).astype(jnp.bfloat16)
    joined, adds = lax.optimization_barrier(
        (joined, (of % depth == to).astype(jnp.bfloat16))
    )
    proj_both = jnp.concatenate(
        [mine(proj, 1, core_head), proj_other, placed(core), placed(1 - core)], axis=0
    )
    partial = matmul(joined, proj_both).astype(jnp.bfloat16)

    chunk = near_sum(partial, adds)
    core_far, chip_far, owner_far, ids_far, bias_far, _ = lax.optimization_barrier(
        (core, chip, owner_map, token_ids, enc_bias, chunk)
    )
    encoder_both = jnp.concatenate(
        [mine(encoder, 0, core_far), other_core(theirs(encoder, 0, core_far))], axis=1
    )
    decoder_both = jnp.concatenate(
        [mine(decoder, 1, core_far), other_core(theirs(decoder, 1, core_far))], axis=0
    )
    my_bias = mine(dec_bias, 0, core_far).astype(jnp.float32)
    across = (
        chip_of(old // block_rows, 1 - core_far) == chip_of(row // block_rows, core_far)
    ) & same_place
    kept = (ids_far.reshape(blocks, block_rows) != BOS).astype(jnp.float32)
    mask_rows = jnp.sum(jnp.where((owner_far == chip_far)[:, None], kept, 0.0), axis=0)[:, None]
    summed, encoder_both, decoder_both, mask_rows, my_bias, across, lat_bias = (
        lax.optimization_barrier(
            (
                far_sum(chunk),
                encoder_both,
                decoder_both,
                mask_rows,
                my_bias,
                across.astype(jnp.float32),
                bias_far.astype(jnp.float32)[:, None],
            )
        )
    )
    values = summed.astype(jnp.bfloat16).astype(jnp.float32)
    squares = jnp.sum(values * values, axis=1, keepdims=True)
    squares = squares + other_core(squares)
    inverse_rms = lax.rsqrt(squares / features + 1e-05)
    my_centred = (values * inverse_rms - my_bias).astype(jnp.bfloat16)
    centred = spread(spread(my_centred, FAR_GROUPS, FAR), NEAR_GROUPS, NEAR)

    exact = dict(precision=lax.Precision.HIGHEST)

    def in_my_order(arrived):
        return matmul(arrived, across, ((1,), (1,)), **exact)

    products = matmul(centred, encoder_both).T
    before_relu = products[:own] + in_my_order(other_core(products[own:]))
    before_relu = before_relu + lat_bias
    latents = jnp.maximum(before_relu, 0.0).astype(jnp.bfloat16)
    across_low = across.astype(jnp.bfloat16)
    latents_other = matmul(other_core(latents), across_low, ((1,), (1,))).astype(jnp.bfloat16)
    latents_both = jnp.concatenate([latents, latents_other], axis=0)
    partial = matmul(latents_both, decoder_both, ((0,), (0,))).astype(jnp.bfloat16)
    chunk = near_sum(partial, adds)
    later, _ = lax.optimization_barrier((centred, chunk))
    centred_other = matmul(
        other_core(later), across_low, ((0,), (1,))
    ).astype(jnp.bfloat16)
    centred_own = later.T
    centred_full = jnp.where(
        core == 0,
        jnp.concatenate([centred_own, centred_other], axis=0),
        jnp.concatenate([centred_other, centred_own], axis=0),
    )
    rebuilt, centred_full = lax.optimization_barrier((far_sum(chunk), centred_full))
    my_error = (mask_rows * (rebuilt - my_centred.astype(jnp.float32))).astype(jnp.bfloat16)
    error_rows, owned_error = lax.optimization_barrier(
        (spread(my_error, FAR_GROUPS, FAR), core_and_section(my_error))
    )
    error = spread(error_rows, NEAR_GROUPS, NEAR)
    step_size = STEP_RATE / tokens

    def stepped(weight, grad):
        return (weight.astype(jnp.float32) - step_size * grad).astype(jnp.bfloat16)

    decoder_own, decoder_other = decoder_both[:own], decoder_both[own:]
    over_features = ((1,), (1,))
    arrived = other_core(matmul(decoder_other, error, over_features))
    backward = matmul(decoder_own, error, over_features) + in_my_order(arrived)
    pre_grad = lax.optimization_barrier(
        jnp.where(before_relu > 0.0, backward, 0.0).astype(jnp.bfloat16)
    )
    back_half = other_core(stepped(decoder_other, matmul(latents_other, error)))
    kept_half = stepped(decoder_own, matmul(latents, error))
    new_encoder = stepped(encoder, matmul(centred_full, pre_grad, over_features))
    new_decoder = jnp.where(
        core == 0,
        jnp.concatenate([kept_half, back_half], axis=1),
        jnp.concatenate([back_half, kept_half], axis=1),
    )
    return (owned_error, new_encoder, new_decoder)


def solution(mesh):
    cut = Mesh(mesh.devices.reshape(SIZES), AXES)
    return jax.shard_map(
        shards,
        mesh=cut,
        in_specs=(
            P(None, TENSOR),
            P("xl", None, TENSOR),
            P("xl", TENSOR, None),
            P(None, AXES),
            P(AXES),
            P(AXES, None),
            P(),
            P(),
            P(),
        ),
        out_specs=(
            P(TENSOR, "xl"),
            P(None, AXES),
            P(AXES, None),
        ),
        check_vma=False,
    )
```

```python
import jax
import jax.numpy as jnp
from jax import lax
from jax.sharding import Mesh
from jax.sharding import PartitionSpec as P

BOS = 128000


STEP_RATE = 0.5

AXES = ("xl", "y", "z", "xh", "c")
SIZES = (2, 4, 8, 2, 2)
TENSOR = ("y", "z", "xh", "c")
NEAR = 8
FAR = 16


def device(x, y, z, c):
    return (((x % 2 * 4 + y) * 8 + z % 8) * 2 + x // 2) * 2 + c


NEAR_GROUPS = [
    [device(x, y, 2 * w + p, 0) for x in range(4) for p in range(2)]
    for y in range(4)
    for w in range(4)
] + [
    [device(x, y, 2 * w + 1 + p, 1) for y in range(4) for p in range(2)]
    for x in range(4)
    for w in range(4)
]
FAR_GROUPS = [
    [device(x, y, 2 * w + p, 0) for y in range(4) for w in range(4)]
    for x in range(4)
    for p in range(2)
] + [
    [device(x, y, 2 * w + 1 + p, 1) for x in range(4) for w in range(4)]
    for y in range(4)
    for p in range(2)
]


def chip_of(slot, core):
    near, far = slot // FAR, slot % FAR
    line, pair, other, deep = near // 2, near % 2, far // 4, far % 4
    x = jnp.where(core == 0, line, other)
    y = jnp.where(core == 0, other, line)
    z = (2 * deep + pair + core) % 8
    return (y * 8 + z) * 4 + x


def exchange(value, swap):
    route = []
    for xl in range(2):
        for y in range(4):
            for z in range(8):
                for xh in range(2):
                    for c in range(2):
                        xl2, c2 = swap(xl, c)
                        route.append(
                            (device(xh * 2 + xl, y, z, c), device(xh * 2 + xl2, y, z, c2))
                        )
    return lax.ppermute(value, AXES, route)


def other_core(value):
    return exchange(value, lambda xl, c: (xl, 1 - c))


def core_and_section(value):
    return exchange(value, lambda xl, c: (c, xl))


def matmul(a, b, dims=((1,), (0,)), **how):
    return lax.dot_general(
        a, b, (dims, ((), ())), preferred_element_type=jnp.float32, **how
    )


def all_to_all(pieces, groups):
    return lax.all_to_all(pieces, AXES, 0, 0, axis_index_groups=groups, tiled=True)


def spread(value, groups, count):
    stacked = jnp.broadcast_to(value[None], (count,) + value.shape)
    return all_to_all(stacked, groups).reshape(-1, value.shape[1])


def near_sum(partial):
    tokens, width = partial.shape
    depth = tokens // NEAR
    pieces = all_to_all(partial.reshape(NEAR, depth, width), NEAR_GROUPS)
    to = lax.broadcasted_iota(jnp.int32, (depth, tokens), 0)
    of = lax.broadcasted_iota(jnp.int32, (depth, tokens), 1)
    adds = (of % depth == to).astype(jnp.bfloat16)
    return matmul(adds, pieces.reshape(tokens, width)).astype(jnp.bfloat16)


def far_sum(chunk):
    pieces = all_to_all(chunk.reshape(FAR, -1, chunk.shape[1]), FAR_GROUPS)
    return jnp.sum(pieces.astype(jnp.float32), axis=0)


def shards(
    resid_in, contexts, out_proj, encoder, enc_bias, decoder, dec_bias, token_ids, owner_map
):
    tokens, width = resid_in.shape
    own, features = decoder.shape
    half = features // 2
    blocks = owner_map.shape[0]
    block_rows = tokens // blocks
    y, z, xh, xl, core = (lax.axis_index(a) for a in ("y", "z", "xh", "xl", "c"))
    chip = (y * 8 + z) * 4 + xh * 2 + xl

    def mine(weight, axis):
        return lax.dynamic_slice_in_dim(weight, core * half, half, axis)

    def theirs(weight, axis):
        return lax.dynamic_slice_in_dim(weight, (1 - core) * half, half, axis)

    proj = out_proj[0]
    proj_other = other_core(theirs(proj, 1))
    context_other = other_core(contexts[0])
    resid_other = other_core(resid_in)

    row = lax.broadcasted_iota(jnp.int32, (tokens, tokens), 0)
    old = lax.broadcasted_iota(jnp.int32, (tokens, tokens), 1)
    same_place = row % block_rows == old % block_rows
    at = chip_of(row // block_rows, core)
    owner_of_row = jnp.repeat(owner_map, block_rows)
    order = ((owner_of_row[None, :] == at) & same_place).astype(jnp.bfloat16)
    across = (chip_of(old // block_rows, 1 - core) == at) & same_place
    kept = (token_ids.reshape(blocks, block_rows) != BOS).astype(jnp.float32)
    mask_rows = jnp.sum(jnp.where((owner_map == chip)[:, None], kept, 0.0), axis=0)[:, None]

    start = ((y * 8 + z) * 2 + xh) * 2 * width
    owns = (start // half == core) & (xl == 0)

    def placed(which):
        column = lax.broadcasted_iota(jnp.int32, (width, half), 1)
        target = lax.broadcasted_iota(jnp.int32, (width, half), 0) + (
            start % half + which * width
        )
        return ((column == target) & owns).astype(jnp.bfloat16)

    joined = matmul(
        order,
        jnp.concatenate([contexts[0], context_other, resid_in, resid_other], axis=1),
    ).astype(jnp.bfloat16)
    joined = lax.optimization_barrier(joined)
    proj_both = jnp.concatenate(
        [mine(proj, 1), proj_other, placed(core), placed(1 - core)], axis=0
    )
    partial = matmul(joined, proj_both).astype(jnp.bfloat16)

    encoder_out, decoder_out, _ = lax.optimization_barrier(
        (theirs(encoder, 0), theirs(decoder, 1), partial)
    )
    encoder_both = jnp.concatenate([mine(encoder, 0), other_core(encoder_out)], axis=1)
    decoder_both = jnp.concatenate([mine(decoder, 1), other_core(decoder_out)], axis=0)
    my_bias = mine(dec_bias, 0).astype(jnp.float32)
    chunk = near_sum(partial)
    chunk, encoder_both, decoder_both, mask_rows, my_bias, across = lax.optimization_barrier(
        (chunk, encoder_both, decoder_both, mask_rows, my_bias, across)
    )
    values = far_sum(chunk).astype(jnp.bfloat16).astype(jnp.float32)
    squares = jnp.sum(values * values, axis=1, keepdims=True)
    squares = squares + other_core(squares)
    inverse_rms = lax.rsqrt(squares / features + 1e-05)
    my_centred = (values * inverse_rms - my_bias).astype(jnp.bfloat16)
    centred = spread(spread(my_centred, FAR_GROUPS, FAR), NEAR_GROUPS, NEAR)

    exact = dict(precision=lax.Precision.HIGHEST)

    def in_my_order(arrived):
        return matmul(arrived, across.astype(jnp.float32), ((1,), (1,)), **exact)

    products = matmul(centred, encoder_both).T
    before_relu = products[:own] + in_my_order(other_core(products[own:]))
    before_relu = before_relu + enc_bias.astype(jnp.float32)[:, None]
    latents = jnp.maximum(before_relu, 0.0).astype(jnp.bfloat16)
    across_low = across.astype(jnp.bfloat16)
    latents_other = matmul(other_core(latents), across_low, ((1,), (1,))).astype(jnp.bfloat16)
    latents_both = jnp.concatenate([latents, latents_other], axis=0)
    partial = matmul(latents_both, decoder_both, ((0,), (0,))).astype(jnp.bfloat16)
    rebuilt = far_sum(near_sum(partial))
    my_error = (mask_rows * (rebuilt - my_centred.astype(jnp.float32))).astype(jnp.bfloat16)
    error_rows = spread(my_error, FAR_GROUPS, FAR)
    later, own_rows, _ = lax.optimization_barrier((centred, my_error, error_rows))
    owned_error = core_and_section(own_rows)
    centred_other = matmul(
        other_core(later), across_low, ((0,), (1,))
    ).astype(jnp.bfloat16)
    centred_own = later.T
    centred_full = jnp.where(
        core == 0,
        jnp.concatenate([centred_own, centred_other], axis=0),
        jnp.concatenate([centred_other, centred_own], axis=0),
    )
    error = spread(error_rows, NEAR_GROUPS, NEAR)
    error, centred_full = lax.optimization_barrier((error, centred_full))
    step_size = STEP_RATE / tokens

    def stepped(weight, grad):
        return (weight.astype(jnp.float32) - step_size * grad).astype(jnp.bfloat16)

    decoder_own, decoder_other = decoder_both[:own], decoder_both[own:]
    over_features = ((1,), (1,))
    arrived = other_core(matmul(decoder_other, error, over_features))
    backward = matmul(decoder_own, error, over_features) + in_my_order(arrived)
    pre_grad = lax.optimization_barrier(
        jnp.where(before_relu > 0.0, backward, 0.0).astype(jnp.bfloat16)
    )
    back_half = other_core(stepped(decoder_other, matmul(latents_other, error)))
    kept_half = stepped(decoder_own, matmul(latents, error))
    new_encoder = stepped(encoder, matmul(centred_full, pre_grad, over_features))
    new_decoder = jnp.where(
        core == 0,
        jnp.concatenate([kept_half, back_half], axis=1),
        jnp.concatenate([back_half, kept_half], axis=1),
    )
    return (owned_error, new_encoder, new_decoder)


def solution(mesh):
    cut = Mesh(mesh.devices.reshape(SIZES), AXES)
    return jax.shard_map(
        shards,
        mesh=cut,
        in_specs=(
            P(None, TENSOR),
            P("xl", None, TENSOR),
            P("xl", TENSOR, None),
            P(None, AXES),
            P(AXES),
            P(AXES, None),
            P(),
            P(),
            P(),
        ),
        out_specs=(
            P(TENSOR, "xl"),
            P(None, AXES),
            P(AXES, None),
        ),
        check_vma=False,
    )
```

```python
import jax
import jax.numpy as jnp
from jax import lax
from jax.sharding import Mesh
from jax.sharding import PartitionSpec as P

BOS = 128000


STEP_RATE = 0.5

AXES = ("xl", "y", "z", "xh", "c")
SIZES = (2, 4, 8, 2, 2)
TENSOR = ("y", "z", "xh", "c")
NEAR = 8
FAR = 16


def device(x, y, z, c):
    return (((x % 2 * 4 + y) * 8 + z % 8) * 2 + x // 2) * 2 + c


NEAR_GROUPS = [
    [device(x, y, 2 * w + p, 0) for x in range(4) for p in range(2)]
    for y in range(4)
    for w in range(4)
] + [
    [device(x, y, 2 * w + 1 + p, 1) for y in range(4) for p in range(2)]
    for x in range(4)
    for w in range(4)
]
FAR_GROUPS = [
    [device(x, y, 2 * w + p, 0) for y in range(4) for w in range(4)]
    for x in range(4)
    for p in range(2)
] + [
    [device(x, y, 2 * w + 1 + p, 1) for x in range(4) for w in range(4)]
    for y in range(4)
    for p in range(2)
]


def chip_of(slot, core):
    near, far = slot // FAR, slot % FAR
    line, pair, other, deep = near // 2, near % 2, far // 4, far % 4
    x = jnp.where(core == 0, line, other)
    y = jnp.where(core == 0, other, line)
    z = (2 * deep + pair + core) % 8
    return (y * 8 + z) * 4 + x


def exchange(value, swap):
    route = []
    for xl in range(2):
        for y in range(4):
            for z in range(8):
                for xh in range(2):
                    for c in range(2):
                        xl2, c2 = swap(xl, c)
                        route.append(
                            (device(xh * 2 + xl, y, z, c), device(xh * 2 + xl2, y, z, c2))
                        )
    return lax.ppermute(value, AXES, route)


def other_core(value):
    return exchange(value, lambda xl, c: (xl, 1 - c))


def core_and_section(value):
    return exchange(value, lambda xl, c: (c, xl))


def matmul(a, b, dims=((1,), (0,)), **how):
    return lax.dot_general(
        a, b, (dims, ((), ())), preferred_element_type=jnp.float32, **how
    )


def all_to_all(pieces, groups):
    return lax.all_to_all(pieces, AXES, 0, 0, axis_index_groups=groups, tiled=True)


def spread(value, groups, count):
    stacked = jnp.broadcast_to(value[None], (count,) + value.shape)
    return all_to_all(stacked, groups).reshape(-1, value.shape[1])


def near_sum(partial):
    tokens, width = partial.shape
    depth = tokens // NEAR
    pieces = all_to_all(partial.reshape(NEAR, depth, width), NEAR_GROUPS)
    to = lax.broadcasted_iota(jnp.int32, (depth, tokens), 0)
    of = lax.broadcasted_iota(jnp.int32, (depth, tokens), 1)
    adds = (of % depth == to).astype(jnp.bfloat16)
    return matmul(adds, pieces.reshape(tokens, width)).astype(jnp.bfloat16)


def far_sum(chunk):
    pieces = all_to_all(chunk.reshape(FAR, -1, chunk.shape[1]), FAR_GROUPS)
    return jnp.sum(pieces.astype(jnp.float32), axis=0)


def shards(
    resid_in, contexts, out_proj, encoder, enc_bias, decoder, dec_bias, token_ids, owner_map
):
    tokens, width = resid_in.shape
    own, features = decoder.shape
    half = features // 2
    blocks = owner_map.shape[0]
    block_rows = tokens // blocks
    y, z, xh, xl, core = (lax.axis_index(a) for a in ("y", "z", "xh", "xl", "c"))
    chip = (y * 8 + z) * 4 + xh * 2 + xl

    def mine(weight, axis):
        return lax.dynamic_slice_in_dim(weight, core * half, half, axis)

    def theirs(weight, axis):
        return lax.dynamic_slice_in_dim(weight, (1 - core) * half, half, axis)

    proj = out_proj[0]
    proj_other = other_core(theirs(proj, 1))
    context_other = other_core(contexts[0])
    resid_other = other_core(resid_in)

    row = lax.broadcasted_iota(jnp.int32, (tokens, tokens), 0)
    old = lax.broadcasted_iota(jnp.int32, (tokens, tokens), 1)
    same_place = row % block_rows == old % block_rows
    at = chip_of(row // block_rows, core)
    owner_of_row = jnp.repeat(owner_map, block_rows)
    order = ((owner_of_row[None, :] == at) & same_place).astype(jnp.bfloat16)
    across = (chip_of(old // block_rows, 1 - core) == at) & same_place
    kept = (token_ids.reshape(blocks, block_rows) != BOS).astype(jnp.float32)
    mask_rows = jnp.sum(jnp.where((owner_map == chip)[:, None], kept, 0.0), axis=0)[:, None]

    start = ((y * 8 + z) * 2 + xh) * 2 * width
    owns = (start // half == core) & (xl == 0)

    def placed(which):
        column = lax.broadcasted_iota(jnp.int32, (width, half), 1)
        target = lax.broadcasted_iota(jnp.int32, (width, half), 0) + (
            start % half + which * width
        )
        return ((column == target) & owns).astype(jnp.bfloat16)

    joined = matmul(
        order,
        jnp.concatenate([contexts[0], resid_in, context_other, resid_other], axis=1),
    ).astype(jnp.bfloat16)
    joined = lax.optimization_barrier(joined)
    proj_both = jnp.concatenate(
        [mine(proj, 1), placed(core), proj_other, placed(1 - core)], axis=0
    )
    partial = matmul(joined, proj_both).astype(jnp.bfloat16)

    encoder_out, decoder_out, _ = lax.optimization_barrier(
        (theirs(encoder, 0), theirs(decoder, 1), partial)
    )
    encoder_both = jnp.concatenate([mine(encoder, 0), other_core(encoder_out)], axis=1)
    decoder_both = jnp.concatenate([mine(decoder, 1), other_core(decoder_out)], axis=0)
    my_bias = mine(dec_bias, 0).astype(jnp.float32)
    chunk = near_sum(partial)
    chunk, encoder_both, decoder_both, mask_rows, my_bias, across = lax.optimization_barrier(
        (chunk, encoder_both, decoder_both, mask_rows, my_bias, across)
    )
    values = far_sum(chunk).astype(jnp.bfloat16).astype(jnp.float32)
    squares = jnp.sum(values * values, axis=1, keepdims=True)
    squares = squares + other_core(squares)
    inverse_rms = lax.rsqrt(squares / features + 1e-05)
    my_centred = (values * inverse_rms - my_bias).astype(jnp.bfloat16)
    centred = spread(spread(my_centred, FAR_GROUPS, FAR), NEAR_GROUPS, NEAR)

    exact = dict(precision=lax.Precision.HIGHEST)

    def in_my_order(arrived):
        return matmul(arrived, across.astype(jnp.float32), ((1,), (1,)), **exact)

    products = matmul(centred, encoder_both).T
    before_relu = products[:own] + in_my_order(other_core(products[own:]))
    before_relu = before_relu + enc_bias.astype(jnp.float32)[:, None]
    latents = jnp.maximum(before_relu, 0.0).astype(jnp.bfloat16)
    across_low = across.astype(jnp.bfloat16)
    latents_other = matmul(other_core(latents), across_low, ((1,), (1,))).astype(jnp.bfloat16)
    latents_both = jnp.concatenate([latents, latents_other], axis=0)
    partial = matmul(latents_both, decoder_both, ((0,), (0,))).astype(jnp.bfloat16)
    rebuilt = far_sum(near_sum(partial))
    my_error = (mask_rows * (rebuilt - my_centred.astype(jnp.float32))).astype(jnp.bfloat16)
    error_rows = spread(my_error, FAR_GROUPS, FAR)
    later, _ = lax.optimization_barrier((centred, error_rows))
    centred_other = matmul(
        other_core(later), across_low, ((0,), (1,))
    ).astype(jnp.bfloat16)
    centred_own = later.T
    centred_full = jnp.where(
        core == 0,
        jnp.concatenate([centred_own, centred_other], axis=0),
        jnp.concatenate([centred_other, centred_own], axis=0),
    )
    own_rows, centred_full = lax.optimization_barrier((my_error, centred_full))
    owned_error = core_and_section(own_rows)
    error = spread(error_rows, NEAR_GROUPS, NEAR)
    error, centred_full = lax.optimization_barrier((error, centred_full))
    step_size = STEP_RATE / tokens

    def stepped(weight, grad):
        return (weight.astype(jnp.float32) - step_size * grad).astype(jnp.bfloat16)

    decoder_own, decoder_other = decoder_both[:own], decoder_both[own:]
    over_features = ((1,), (1,))
    sent = matmul(decoder_other, error, over_features)
    arrived = other_core(sent)
    error, _ = lax.optimization_barrier((error, sent))
    backward = matmul(decoder_own, error, over_features) + in_my_order(arrived)
    pre_grad = lax.optimization_barrier(
        jnp.where(before_relu > 0.0, backward, 0.0).astype(jnp.bfloat16)
    )
    back_half = other_core(stepped(decoder_other, matmul(latents_other, error)))
    kept_half = stepped(decoder_own, matmul(latents, error))
    new_encoder = stepped(encoder, matmul(centred_full, pre_grad, over_features))
    new_decoder = jnp.where(
        core == 0,
        jnp.concatenate([kept_half, back_half], axis=1),
        jnp.concatenate([back_half, kept_half], axis=1),
    )
    return (owned_error, new_encoder, new_decoder)


def solution(mesh):
    cut = Mesh(mesh.devices.reshape(SIZES), AXES)
    return jax.shard_map(
        shards,
        mesh=cut,
        in_specs=(
            P(None, TENSOR),
            P("xl", None, TENSOR),
            P("xl", TENSOR, None),
            P(None, AXES),
            P(AXES),
            P(AXES, None),
            P(),
            P(),
            P(),
        ),
        out_specs=(
            P(TENSOR, "xl"),
            P(None, AXES),
            P(AXES, None),
        ),
        check_vma=False,
    )
```

```python
import jax
import jax.numpy as jnp
from jax import lax
from jax.sharding import Mesh
from jax.sharding import PartitionSpec as P

BOS = 128000


STEP_RATE = 0.5

AXES = ("xl", "y", "z", "xh", "c")
SIZES = (2, 4, 8, 2, 2)
TENSOR = ("y", "z", "xh", "c")
NEAR = 8
FAR = 16


def device(x, y, z, c):
    return (((x % 2 * 4 + y) * 8 + z % 8) * 2 + x // 2) * 2 + c


NEAR_GROUPS = [
    [device(x, y, 2 * w + p, 0) for x in range(4) for p in range(2)]
    for y in range(4)
    for w in range(4)
] + [
    [device(x, y, 2 * w + 1 + p, 1) for y in range(4) for p in range(2)]
    for x in range(4)
    for w in range(4)
]
FAR_GROUPS = [
    [device(x, y, 2 * w + p, 0) for y in range(4) for w in range(4)]
    for x in range(4)
    for p in range(2)
] + [
    [device(x, y, 2 * w + 1 + p, 1) for x in range(4) for w in range(4)]
    for y in range(4)
    for p in range(2)
]


def chip_of(slot, core):
    near, far = slot // FAR, slot % FAR
    line, pair, other, deep = near // 2, near % 2, far // 4, far % 4
    x = jnp.where(core == 0, line, other)
    y = jnp.where(core == 0, other, line)
    z = (2 * deep + pair + core) % 8
    return (y * 8 + z) * 4 + x


def exchange(value, swap):
    route = []
    for xl in range(2):
        for y in range(4):
            for z in range(8):
                for xh in range(2):
                    for c in range(2):
                        xl2, c2 = swap(xl, c)
                        route.append(
                            (device(xh * 2 + xl, y, z, c), device(xh * 2 + xl2, y, z, c2))
                        )
    return lax.ppermute(value, AXES, route)


def other_core(value):
    return exchange(value, lambda xl, c: (xl, 1 - c))


def core_and_section(value):
    return exchange(value, lambda xl, c: (c, xl))


def matmul(a, b, dims=((1,), (0,)), **how):
    return lax.dot_general(
        a, b, (dims, ((), ())), preferred_element_type=jnp.float32, **how
    )


def all_to_all(pieces, groups):
    return lax.all_to_all(pieces, AXES, 0, 0, axis_index_groups=groups, tiled=True)


def spread(value, groups, count):
    stacked = jnp.broadcast_to(value[None], (count,) + value.shape)
    return all_to_all(stacked, groups).reshape(-1, value.shape[1])


def near_sum(partial):
    tokens, width = partial.shape
    depth = tokens // NEAR
    pieces = all_to_all(partial.reshape(NEAR, depth, width), NEAR_GROUPS)
    to = lax.broadcasted_iota(jnp.int32, (depth, tokens), 0)
    of = lax.broadcasted_iota(jnp.int32, (depth, tokens), 1)
    adds = (of % depth == to).astype(jnp.bfloat16)
    return matmul(adds, pieces.reshape(tokens, width)).astype(jnp.bfloat16)


def far_sum(chunk):
    pieces = all_to_all(chunk.reshape(FAR, -1, chunk.shape[1]), FAR_GROUPS)
    return jnp.sum(pieces.astype(jnp.float32), axis=0)


def shards(
    resid_in, contexts, out_proj, encoder, enc_bias, decoder, dec_bias, token_ids, owner_map
):
    tokens, width = resid_in.shape
    own, features = decoder.shape
    half = features // 2
    blocks = owner_map.shape[0]
    block_rows = tokens // blocks
    y, z, xh, xl, core = (lax.axis_index(a) for a in ("y", "z", "xh", "xl", "c"))
    chip = (y * 8 + z) * 4 + xh * 2 + xl

    def mine(weight, axis):
        return lax.dynamic_slice_in_dim(weight, core * half, half, axis)

    def theirs(weight, axis):
        return lax.dynamic_slice_in_dim(weight, (1 - core) * half, half, axis)

    proj = out_proj[0]
    proj_other = other_core(theirs(proj, 1))

    row = lax.broadcasted_iota(jnp.int32, (tokens, tokens), 0)
    old = lax.broadcasted_iota(jnp.int32, (tokens, tokens), 1)
    same_place = row % block_rows == old % block_rows
    at = chip_of(row // block_rows, core)
    at_other = chip_of(row // block_rows, 1 - core)
    owner_of_row = jnp.repeat(owner_map, block_rows)
    orders = [
        ((owner_of_row[None, :] == to) & same_place).astype(jnp.bfloat16)
        for to in (at, at_other)
    ]
    across = (chip_of(old // block_rows, 1 - core) == at) & same_place
    kept = (token_ids.reshape(blocks, block_rows) != BOS).astype(jnp.float32)
    mask_rows = jnp.sum(jnp.where((owner_map == chip)[:, None], kept, 0.0), axis=0)[:, None]

    start = ((y * 8 + z) * 2 + xh) * 2 * width
    owns = (start // half == core) & (xl == 0)

    def placed(which):
        column = lax.broadcasted_iota(jnp.int32, (width, half), 1)
        target = lax.broadcasted_iota(jnp.int32, (width, half), 0) + (
            start % half + which * width
        )
        return ((column == target) & owns).astype(jnp.bfloat16)

    given = jnp.concatenate([contexts[0], resid_in], axis=1)
    joined, joined_out = lax.optimization_barrier(
        [matmul(order, given).astype(jnp.bfloat16) for order in orders]
    )
    joined = jnp.concatenate([joined, other_core(joined_out)], axis=1)
    proj_both = jnp.concatenate(
        [mine(proj, 1), placed(core), proj_other, placed(1 - core)], axis=0
    )
    partial = matmul(joined, proj_both).astype(jnp.bfloat16)

    encoder_out, decoder_out, _ = lax.optimization_barrier(
        (theirs(encoder, 0), theirs(decoder, 1), partial)
    )
    encoder_both = jnp.concatenate([mine(encoder, 0), other_core(encoder_out)], axis=1)
    decoder_both = jnp.concatenate([mine(decoder, 1), other_core(decoder_out)], axis=0)
    my_bias = mine(dec_bias, 0).astype(jnp.float32)
    chunk = near_sum(partial)
    chunk, encoder_both, decoder_both, mask_rows, my_bias, across = lax.optimization_barrier(
        (chunk, encoder_both, decoder_both, mask_rows, my_bias, across)
    )
    values = far_sum(chunk).astype(jnp.bfloat16).astype(jnp.float32)
    squares = jnp.sum(values * values, axis=1, keepdims=True)
    squares = squares + other_core(squares)
    inverse_rms = lax.rsqrt(squares / features + 1e-05)
    my_centred = (values * inverse_rms - my_bias).astype(jnp.bfloat16)
    centred = spread(spread(my_centred, FAR_GROUPS, FAR), NEAR_GROUPS, NEAR)

    exact = dict(precision=lax.Precision.HIGHEST)

    def in_my_order(arrived):
        return matmul(arrived, across.astype(jnp.float32), ((1,), (1,)), **exact)

    products = matmul(centred, encoder_both).T
    before_relu = products[:own] + in_my_order(other_core(products[own:]))
    before_relu = before_relu + enc_bias.astype(jnp.float32)[:, None]
    latents = jnp.maximum(before_relu, 0.0).astype(jnp.bfloat16)
    across_low = across.astype(jnp.bfloat16)
    latents_other = matmul(other_core(latents), across_low, ((1,), (1,))).astype(jnp.bfloat16)
    latents_both = jnp.concatenate([latents, latents_other], axis=0)
    partial = matmul(latents_both, decoder_both, ((0,), (0,))).astype(jnp.bfloat16)
    rebuilt = far_sum(near_sum(partial))
    my_error = (mask_rows * (rebuilt - my_centred.astype(jnp.float32))).astype(jnp.bfloat16)
    error_rows = spread(my_error, FAR_GROUPS, FAR)
    later, _ = lax.optimization_barrier((centred, error_rows))
    centred_other = matmul(
        other_core(later), across_low, ((0,), (1,))
    ).astype(jnp.bfloat16)
    centred_own = later.T
    centred_full = jnp.where(
        core == 0,
        jnp.concatenate([centred_own, centred_other], axis=0),
        jnp.concatenate([centred_other, centred_own], axis=0),
    )
    own_rows, centred_full = lax.optimization_barrier((my_error, centred_full))
    owned_error = core_and_section(own_rows)
    error = spread(error_rows, NEAR_GROUPS, NEAR)
    error, centred_full = lax.optimization_barrier((error, centred_full))
    step_size = STEP_RATE / tokens

    def stepped(weight, grad):
        return (weight.astype(jnp.float32) - step_size * grad).astype(jnp.bfloat16)

    decoder_own, decoder_other = decoder_both[:own], decoder_both[own:]
    over_features = ((1,), (1,))
    sent = matmul(decoder_other, error, over_features)
    arrived = other_core(sent)
    error, _ = lax.optimization_barrier((error, sent))
    backward = matmul(decoder_own, error, over_features) + in_my_order(arrived)
    pre_grad = lax.optimization_barrier(
        jnp.where(before_relu > 0.0, backward, 0.0).astype(jnp.bfloat16)
    )
    back_half = other_core(stepped(decoder_other, matmul(latents_other, error)))
    kept_half = stepped(decoder_own, matmul(latents, error))
    new_decoder = jnp.where(
        core == 0,
        jnp.concatenate([kept_half, back_half], axis=1),
        jnp.concatenate([back_half, kept_half], axis=1),
    )
    pre_grad, _ = lax.optimization_barrier((pre_grad, new_decoder))
    new_encoder = stepped(encoder, matmul(centred_full, pre_grad, over_features))
    return (owned_error, new_encoder, new_decoder)


def solution(mesh):
    cut = Mesh(mesh.devices.reshape(SIZES), AXES)
    return jax.shard_map(
        shards,
        mesh=cut,
        in_specs=(
            P(None, TENSOR),
            P("xl", None, TENSOR),
            P("xl", TENSOR, None),
            P(None, AXES),
            P(AXES),
            P(AXES, None),
            P(),
            P(),
            P(),
        ),
        out_specs=(
            P(TENSOR, "xl"),
            P(None, AXES),
            P(AXES, None),
        ),
        check_vma=False,
    )
```

```python
import jax
import jax.numpy as jnp
from jax import lax
from jax.sharding import Mesh
from jax.sharding import PartitionSpec as P

BOS = 128000


STEP_RATE = 0.5

AXES = ("xl", "y", "z", "xh", "c")
SIZES = (2, 4, 8, 2, 2)
TENSOR = ("y", "z", "xh", "c")
NEAR = 8
FAR = 16


def device(x, y, z, c):
    return (((x % 2 * 4 + y) * 8 + z % 8) * 2 + x // 2) * 2 + c


NEAR_GROUPS = [
    [device(x, y, 2 * w + p, 0) for x in range(4) for p in range(2)]
    for y in range(4)
    for w in range(4)
] + [
    [device(x, y, 2 * w + 1 + p, 1) for y in range(4) for p in range(2)]
    for x in range(4)
    for w in range(4)
]
FAR_GROUPS = [
    [device(x, y, 2 * w + p, 0) for y in range(4) for w in range(4)]
    for x in range(4)
    for p in range(2)
] + [
    [device(x, y, 2 * w + 1 + p, 1) for x in range(4) for w in range(4)]
    for y in range(4)
    for p in range(2)
]


def chip_of(slot, core):
    near, far = slot // FAR, slot % FAR
    line, pair, other, deep = near // 2, near % 2, far // 4, far % 4
    x = jnp.where(core == 0, line, other)
    y = jnp.where(core == 0, other, line)
    z = (2 * deep + pair + core) % 8
    return (y * 8 + z) * 4 + x


def exchange(value, swap):
    route = []
    for xl in range(2):
        for y in range(4):
            for z in range(8):
                for xh in range(2):
                    for c in range(2):
                        xl2, c2 = swap(xl, c)
                        route.append(
                            (device(xh * 2 + xl, y, z, c), device(xh * 2 + xl2, y, z, c2))
                        )
    return lax.ppermute(value, AXES, route)


def other_core(value):
    return exchange(value, lambda xl, c: (xl, 1 - c))


def core_and_section(value):
    return exchange(value, lambda xl, c: (c, xl))


def matmul(a, b, dims=((1,), (0,)), **how):
    return lax.dot_general(
        a, b, (dims, ((), ())), preferred_element_type=jnp.float32, **how
    )


def all_to_all(pieces, groups):
    return lax.all_to_all(pieces, AXES, 0, 0, axis_index_groups=groups, tiled=True)


def spread(value, groups, count):
    stacked = jnp.broadcast_to(value[None], (count,) + value.shape)
    return all_to_all(stacked, groups).reshape(-1, value.shape[1])


def near_sum(partial):
    tokens, width = partial.shape
    depth = tokens // NEAR
    pieces = all_to_all(partial.reshape(NEAR, depth, width), NEAR_GROUPS)
    to = lax.broadcasted_iota(jnp.int32, (depth, tokens), 0)
    of = lax.broadcasted_iota(jnp.int32, (depth, tokens), 1)
    adds = (of % depth == to).astype(jnp.bfloat16)
    return matmul(adds, pieces.reshape(tokens, width)).astype(jnp.bfloat16)


def far_sum(chunk):
    pieces = all_to_all(chunk.reshape(FAR, -1, chunk.shape[1]), FAR_GROUPS)
    return jnp.sum(pieces.astype(jnp.float32), axis=0)


def shards(
    resid_in, contexts, out_proj, encoder, enc_bias, decoder, dec_bias, token_ids, owner_map
):
    tokens, width = resid_in.shape
    own, features = decoder.shape
    half = features // 2
    blocks = owner_map.shape[0]
    block_rows = tokens // blocks
    y, z, xh, xl, core = (lax.axis_index(a) for a in ("y", "z", "xh", "xl", "c"))
    chip = (y * 8 + z) * 4 + xh * 2 + xl

    def mine(weight, axis):
        return lax.dynamic_slice_in_dim(weight, core * half, half, axis)

    def theirs(weight, axis):
        return lax.dynamic_slice_in_dim(weight, (1 - core) * half, half, axis)

    proj = out_proj[0]
    proj_other = other_core(theirs(proj, 1))

    row = lax.broadcasted_iota(jnp.int32, (tokens, tokens), 0)
    old = lax.broadcasted_iota(jnp.int32, (tokens, tokens), 1)
    same_place = row % block_rows == old % block_rows
    at = chip_of(row // block_rows, core)
    at_other = chip_of(row // block_rows, 1 - core)
    owner_of_row = jnp.repeat(owner_map, block_rows)
    orders = [
        ((owner_of_row[None, :] == to) & same_place).astype(jnp.bfloat16)
        for to in (at, at_other)
    ]
    across = (chip_of(old // block_rows, 1 - core) == at) & same_place
    kept = (token_ids.reshape(blocks, block_rows) != BOS).astype(jnp.float32)
    mask_rows = jnp.sum(jnp.where((owner_map == chip)[:, None], kept, 0.0), axis=0)[:, None]

    start = ((y * 8 + z) * 2 + xh) * 2 * width
    owns = (start // half == core) & (xl == 0)

    def placed(which):
        column = lax.broadcasted_iota(jnp.int32, (width, half), 1)
        target = lax.broadcasted_iota(jnp.int32, (width, half), 0) + (
            start % half + which * width
        )
        return ((column == target) & owns).astype(jnp.bfloat16)

    given = jnp.concatenate([contexts[0], resid_in], axis=1)
    joined, joined_out = lax.optimization_barrier(
        [matmul(order, given).astype(jnp.bfloat16) for order in orders]
    )
    joined = jnp.concatenate([joined, other_core(joined_out)], axis=1)
    proj_both = jnp.concatenate(
        [mine(proj, 1), placed(core), proj_other, placed(1 - core)], axis=0
    )
    partial = matmul(joined, proj_both).astype(jnp.bfloat16)

    encoder_out, decoder_out, _ = lax.optimization_barrier(
        (theirs(encoder, 0), theirs(decoder, 1), partial)
    )
    encoder_both = jnp.concatenate([mine(encoder, 0), other_core(encoder_out)], axis=1)
    decoder_both = jnp.concatenate([mine(decoder, 1), other_core(decoder_out)], axis=0)
    my_bias = mine(dec_bias, 0).astype(jnp.float32)
    chunk = near_sum(partial)
    chunk, encoder_both, decoder_both, mask_rows, my_bias, across = lax.optimization_barrier(
        (chunk, encoder_both, decoder_both, mask_rows, my_bias, across)
    )
    values = far_sum(chunk).astype(jnp.bfloat16).astype(jnp.float32)
    squares = jnp.sum(values * values, axis=1, keepdims=True)
    squares = squares + other_core(squares)
    inverse_rms = lax.rsqrt(squares / features + 1e-05)
    my_centred = (values * inverse_rms - my_bias).astype(jnp.bfloat16)
    centred = spread(spread(my_centred, FAR_GROUPS, FAR), NEAR_GROUPS, NEAR)

    exact = dict(precision=lax.Precision.HIGHEST)

    def in_my_order(arrived):
        return matmul(arrived, across.astype(jnp.float32), ((1,), (1,)), **exact)

    products = matmul(centred, encoder_both).T
    before_relu = products[:own] + in_my_order(other_core(products[own:]))
    before_relu = before_relu + enc_bias.astype(jnp.float32)[:, None]
    latents = jnp.maximum(before_relu, 0.0).astype(jnp.bfloat16)
    across_low = across.astype(jnp.bfloat16)
    latents_other = matmul(other_core(latents), across_low, ((1,), (1,))).astype(jnp.bfloat16)
    latents_both = jnp.concatenate([latents, latents_other], axis=0)
    partial = matmul(latents_both, decoder_both, ((0,), (0,))).astype(jnp.bfloat16)
    rebuilt = far_sum(near_sum(partial))
    my_error = (mask_rows * (rebuilt - my_centred.astype(jnp.float32))).astype(jnp.bfloat16)
    error_rows = spread(my_error, FAR_GROUPS, FAR)
    later, _ = lax.optimization_barrier((centred, error_rows))
    centred_other = matmul(
        other_core(later), across_low, ((0,), (1,))
    ).astype(jnp.bfloat16)
    centred_own = later.T
    centred_full = jnp.where(
        core == 0,
        jnp.concatenate([centred_own, centred_other], axis=0),
        jnp.concatenate([centred_other, centred_own], axis=0),
    )
    own_rows, centred_full = lax.optimization_barrier((my_error, centred_full))
    owned_error = core_and_section(own_rows)
    error = spread(error_rows, NEAR_GROUPS, NEAR)
    error, centred_full, owned_error = lax.optimization_barrier(
        (error, centred_full, owned_error)
    )
    step_size = STEP_RATE / tokens

    def stepped(weight, grad):
        return (weight.astype(jnp.float32) - step_size * grad).astype(jnp.bfloat16)

    decoder_own, decoder_other = decoder_both[:own], decoder_both[own:]
    over_features = ((1,), (1,))
    sent = matmul(decoder_other, error, over_features)
    arrived = other_core(sent)
    error, _ = lax.optimization_barrier((error, sent))
    backward = matmul(decoder_own, error, over_features) + in_my_order(arrived)
    pre_grad = lax.optimization_barrier(
        jnp.where(before_relu > 0.0, backward, 0.0).astype(jnp.bfloat16)
    )
    back_half = other_core(stepped(decoder_other, matmul(latents_other, error)))
    kept_half = stepped(decoder_own, matmul(latents, error))
    new_encoder = stepped(encoder, matmul(centred_full, pre_grad, over_features))
    new_decoder = jnp.where(
        core == 0,
        jnp.concatenate([kept_half, back_half], axis=1),
        jnp.concatenate([back_half, kept_half], axis=1),
    )
    return (owned_error, new_encoder, new_decoder)


def solution(mesh):
    cut = Mesh(mesh.devices.reshape(SIZES), AXES)
    return jax.shard_map(
        shards,
        mesh=cut,
        in_specs=(
            P(None, TENSOR),
            P("xl", None, TENSOR),
            P("xl", TENSOR, None),
            P(None, AXES),
            P(AXES),
            P(AXES, None),
            P(),
            P(),
            P(),
        ),
        out_specs=(
            P(TENSOR, "xl"),
            P(None, AXES),
            P(AXES, None),
        ),
        check_vma=False,
    )
```

```python
import jax
import jax.numpy as jnp
from jax import lax
from jax.sharding import Mesh
from jax.sharding import PartitionSpec as P

BOS = 128000


STEP_RATE = 0.5

AXES = ("xl", "y", "z", "xh", "c")
SIZES = (2, 4, 8, 2, 2)
TENSOR = ("y", "z", "xh", "c")
NEAR = 8
FAR = 16


def device(x, y, z, c):
    return (((x % 2 * 4 + y) * 8 + z % 8) * 2 + x // 2) * 2 + c


NEAR_GROUPS = [
    [device(x, y, 2 * w + p, 0) for x in range(4) for p in range(2)]
    for y in range(4)
    for w in range(4)
] + [
    [device(x, y, 2 * w + 1 + p, 1) for y in range(4) for p in range(2)]
    for x in range(4)
    for w in range(4)
]
FAR_GROUPS = [
    [device(x, y, 2 * w + p, 0) for y in range(4) for w in range(4)]
    for x in range(4)
    for p in range(2)
] + [
    [device(x, y, 2 * w + 1 + p, 1) for x in range(4) for w in range(4)]
    for y in range(4)
    for p in range(2)
]


def chip_of(slot, core):
    near, far = slot // FAR, slot % FAR
    line, pair, other, deep = near // 2, near % 2, far // 4, far % 4
    x = jnp.where(core == 0, line, other)
    y = jnp.where(core == 0, other, line)
    z = (2 * deep + pair + core) % 8
    return (y * 8 + z) * 4 + x


def exchange(value, swap):
    route = []
    for xl in range(2):
        for y in range(4):
            for z in range(8):
                for xh in range(2):
                    for c in range(2):
                        xl2, c2 = swap(xl, c)
                        route.append(
                            (device(xh * 2 + xl, y, z, c), device(xh * 2 + xl2, y, z, c2))
                        )
    return lax.ppermute(value, AXES, route)


def other_core(value):
    return exchange(value, lambda xl, c: (xl, 1 - c))


def core_and_section(value):
    return exchange(value, lambda xl, c: (c, xl))


def matmul(a, b, dims=((1,), (0,)), **how):
    return lax.dot_general(
        a, b, (dims, ((), ())), preferred_element_type=jnp.float32, **how
    )


def all_to_all(pieces, groups):
    return lax.all_to_all(pieces, AXES, 0, 0, axis_index_groups=groups, tiled=True)


def spread(value, groups, count):
    stacked = jnp.broadcast_to(value[None], (count,) + value.shape)
    return all_to_all(stacked, groups).reshape(-1, value.shape[1])


def near_sum(partial):
    tokens, width = partial.shape
    depth = tokens // NEAR
    pieces = all_to_all(partial.reshape(NEAR, depth, width), NEAR_GROUPS)
    to = lax.broadcasted_iota(jnp.int32, (depth, tokens), 0)
    of = lax.broadcasted_iota(jnp.int32, (depth, tokens), 1)
    adds = (of % depth == to).astype(jnp.bfloat16)
    return matmul(adds, pieces.reshape(tokens, width)).astype(jnp.bfloat16)


def far_sum(chunk):
    pieces = all_to_all(chunk.reshape(FAR, -1, chunk.shape[1]), FAR_GROUPS)
    return jnp.sum(pieces.astype(jnp.float32), axis=0)


def shards(
    resid_in, contexts, out_proj, encoder, enc_bias, decoder, dec_bias, token_ids, owner_map
):
    tokens, width = resid_in.shape
    own, features = decoder.shape
    half = features // 2
    blocks = owner_map.shape[0]
    block_rows = tokens // blocks
    y, z, xh, xl, core = (lax.axis_index(a) for a in ("y", "z", "xh", "xl", "c"))
    chip = (y * 8 + z) * 4 + xh * 2 + xl

    def mine(weight, axis):
        return lax.dynamic_slice_in_dim(weight, core * half, half, axis)

    def theirs(weight, axis):
        return lax.dynamic_slice_in_dim(weight, (1 - core) * half, half, axis)

    proj = out_proj[0]
    proj_other = other_core(theirs(proj, 1))

    row = lax.broadcasted_iota(jnp.int32, (tokens, tokens), 0)
    old = lax.broadcasted_iota(jnp.int32, (tokens, tokens), 1)
    same_place = row % block_rows == old % block_rows
    at = chip_of(row // block_rows, core)
    at_other = chip_of(row // block_rows, 1 - core)
    owner_of_row = jnp.repeat(owner_map, block_rows)
    orders = [
        ((owner_of_row[None, :] == to) & same_place).astype(jnp.bfloat16)
        for to in (at, at_other)
    ]
    across = (chip_of(old // block_rows, 1 - core) == at) & same_place
    kept = (token_ids.reshape(blocks, block_rows) != BOS).astype(jnp.float32)
    mask_rows = jnp.sum(jnp.where((owner_map == chip)[:, None], kept, 0.0), axis=0)[:, None]

    start = ((y * 8 + z) * 2 + xh) * 2 * width
    owns = (start // half == core) & (xl == 0)

    def placed(which):
        column = lax.broadcasted_iota(jnp.int32, (width, half), 1)
        target = lax.broadcasted_iota(jnp.int32, (width, half), 0) + (
            start % half + which * width
        )
        return ((column == target) & owns).astype(jnp.bfloat16)

    given = jnp.concatenate([contexts[0], resid_in], axis=1)
    joined, joined_out = lax.optimization_barrier(
        [matmul(order, given).astype(jnp.bfloat16) for order in orders]
    )
    joined = jnp.concatenate([joined, other_core(joined_out)], axis=1)
    proj_both = jnp.concatenate(
        [mine(proj, 1), placed(core), proj_other, placed(1 - core)], axis=0
    )
    partial = matmul(joined, proj_both).astype(jnp.bfloat16)

    encoder_out, decoder_out, _ = lax.optimization_barrier(
        (theirs(encoder, 0), theirs(decoder, 1), partial)
    )
    encoder_both = jnp.concatenate([mine(encoder, 0), other_core(encoder_out)], axis=1)
    decoder_both = jnp.concatenate([mine(decoder, 1), other_core(decoder_out)], axis=0)
    my_bias = mine(dec_bias, 0).astype(jnp.float32)
    chunk = near_sum(partial)
    chunk, encoder_both, decoder_both, mask_rows, my_bias, across = lax.optimization_barrier(
        (chunk, encoder_both, decoder_both, mask_rows, my_bias, across)
    )
    values = far_sum(chunk).astype(jnp.bfloat16).astype(jnp.float32)
    squares = jnp.sum(values * values, axis=1, keepdims=True)
    squares = squares + other_core(squares)
    inverse_rms = lax.rsqrt(squares / features + 1e-05)
    my_centred = (values * inverse_rms - my_bias).astype(jnp.bfloat16)
    centred = spread(spread(my_centred, FAR_GROUPS, FAR), NEAR_GROUPS, NEAR)

    exact = dict(precision=lax.Precision.HIGHEST)

    def in_my_order(arrived):
        return matmul(arrived, across.astype(jnp.float32), ((1,), (1,)), **exact)

    products = matmul(centred, encoder_both).T
    before_relu = products[:own] + in_my_order(other_core(products[own:]))
    before_relu = before_relu + enc_bias.astype(jnp.float32)[:, None]
    latents = jnp.maximum(before_relu, 0.0).astype(jnp.bfloat16)
    across_low = across.astype(jnp.bfloat16)
    latents_other = matmul(other_core(latents), across_low, ((1,), (1,))).astype(jnp.bfloat16)
    latents_both = jnp.concatenate([latents, latents_other], axis=0)
    partial = matmul(latents_both, decoder_both, ((0,), (0,))).astype(jnp.bfloat16)
    rebuilt = far_sum(near_sum(partial))
    my_error = (mask_rows * (rebuilt - my_centred.astype(jnp.float32))).astype(jnp.bfloat16)
    error_rows = spread(my_error, FAR_GROUPS, FAR)
    later, _ = lax.optimization_barrier((centred, error_rows))
    centred_other = matmul(
        other_core(later), across_low, ((0,), (1,))
    ).astype(jnp.bfloat16)
    centred_own = later.T
    centred_full = jnp.where(
        core == 0,
        jnp.concatenate([centred_own, centred_other], axis=0),
        jnp.concatenate([centred_other, centred_own], axis=0),
    )
    own_rows, centred_full = lax.optimization_barrier((my_error, centred_full))
    owned_error = core_and_section(own_rows)
    error = spread(error_rows, NEAR_GROUPS, NEAR)
    error, centred_full = lax.optimization_barrier((error, centred_full))
    step_size = STEP_RATE / tokens

    def stepped(weight, grad):
        return (weight.astype(jnp.float32) - step_size * grad).astype(jnp.bfloat16)

    decoder_own, decoder_other = decoder_both[:own], decoder_both[own:]
    over_features = ((1,), (1,))
    sent = matmul(decoder_other, error, over_features)
    arrived = other_core(sent)
    error, _ = lax.optimization_barrier((error, sent))
    backward = matmul(decoder_own, error, over_features) + in_my_order(arrived)
    pre_grad = lax.optimization_barrier(
        jnp.where(before_relu > 0.0, backward, 0.0).astype(jnp.bfloat16)
    )
    back_half = other_core(stepped(decoder_other, matmul(latents_other, error)))
    kept_half = stepped(decoder_own, matmul(latents, error))
    new_encoder = stepped(encoder, matmul(centred_full, pre_grad, over_features))
    new_decoder = jnp.where(
        core == 0,
        jnp.concatenate([kept_half, back_half], axis=1),
        jnp.concatenate([back_half, kept_half], axis=1),
    )
    return (owned_error, new_encoder, new_decoder)


def solution(mesh):
    cut = Mesh(mesh.devices.reshape(SIZES), AXES)
    return jax.shard_map(
        shards,
        mesh=cut,
        in_specs=(
            P(None, TENSOR),
            P("xl", None, TENSOR),
            P("xl", TENSOR, None),
            P(None, AXES),
            P(AXES),
            P(AXES, None),
            P(),
            P(),
            P(),
        ),
        out_specs=(
            P(TENSOR, "xl"),
            P(None, AXES),
            P(AXES, None),
        ),
        check_vma=False,
    )
```
